32 devices in a mesh: gx: 4 (over z), gy: 2 (over y), gz: 4 (over x, core).
Axes of the slice: x: 2, y: 2, z: 4, core: 2. Of those that a mesh axis runs over, the one named last changes fastest.
Arguments:
- residual: float32 [64, 32, 512], P('gx', 'gy', 'gz'), may hold values from -6 to 6
- solution: float32 [64, 32, 512], P('gx', 'gy', 'gz'), may hold values from -6 to 6
- direction: float32 [64, 32, 512], P('gx', 'gy', 'gz'), may hold values from -6 to 6
- conductance: float32 [3, 64, 32, 512], P(None, 'gx', 'gy', 'gz'), may hold values from 0.3 to 3
- mass_term: float32 [64, 32, 512], P('gx', 'gy', 'gz'), may hold values from 0.2 to 1
- eigen_basis: float32 [10, 10], replicated, may hold values from -2 to 2
- inverse_eigen_sums: float32 [80, 40, 640], P('gx', 'gy', 'gz'), may hold values from 0.1 to 1
- element_coarse_index: int32 [8, 4, 64], P('gx', 'gy', 'gz'), may hold values from 0 to 63
- xxt_values: float32 [256, 64, 128], P(('gx', 'gy', 'gz')), may hold values from -0.0625 to 0.0625
- xxt_blocks: int32 [256], P(('gx', 'gy', 'gz')), may hold values from 0 to 15
- prior_inner: float32 [1], replicated, may hold values from 409600 to 1638400
Outputs:
- new_solution: float32 [64, 32, 512], P('gx', 'gy', 'gz')
- new_residual: float32 [64, 32, 512], P('gx', 'gy', 'gz')
- new_direction: float32 [64, 32, 512], P('gx', 'gy', 'gz')
The draws below stay inside these ranges and needn't reach their ends.
Inputs may be any that keep to these rules, and one draw needn't show every extreme that they name: `element_coarse_index`: an element's coarse unknown is one of the 64 of the device that holds the element. `xxt_blocks`: block numbers of the coarse vector, repeats allowed.
All inputs are finite; a program needn't handle non-finite values.
Results may differ from the reference program's by a relative error of at most 0.00011.
Values sent between devices are 32-bit elements; how exact they have to be, the bound alone decides.
A program may use at most 64 MiB of HBM per device.

```python
import math
import jax
import jax.numpy as jnp
import numpy as np
from jax import lax

ELEMENT_NODES = 8
EX = 2
EY = 2
DEVICE_DEPTH_ELS = 16
DEVICE_COARSE = 64
BS = 128
XB = 8
LENGTH_ELEMENTS = 8
ACROSS_ELEMENTS = 4
DEPTH_ELEMENTS = 64
LENGTH_NODES = 64
ACROSS_NODES = 32
DEPTH_NODES = 512
NC = 2048
NB = 16
N_GX = 4
N_GY = 2
N_GZ = 4
DEVICES = 32


def touch_ends(values, own_key, least, largest):
    place = [jax.random.randint(jax.random.fold_in(own_key, axis), (), 0, length) for axis, length in enumerate(values.shape)]
    main_axis = values.shape.index(max(values.shape))
    neighbour = place[:main_axis] + [(place[main_axis] + 1) % values.shape[main_axis]] + place[main_axis + 1:]
    return values.at[tuple(place)].set(least).at[tuple(neighbour)].set(largest)


def shard_levels(rng, dims, pieces, smallest, top_value):
    loudness = 1.0
    for axis_at, shards_of in pieces:
        steps = jax.random.uniform(jax.random.fold_in(jax.random.fold_in(rng, 6), axis_at), (shards_of,), jnp.float32, smallest / len(pieces), top_value / len(pieces))
        loudness = loudness * jnp.repeat(jnp.exp(steps), dims[axis_at] // shards_of).reshape((-1,) + (1,) * (len(dims) - 1 - axis_at))
    return loudness


def normal_values(key, extent, width, limit, split=(), kind=jnp.bfloat16):
    drawn = jax.random.normal(key, extent, jnp.float32) * width
    if len(split) > 0:
        drawn = shard_levels(key, extent, split, -0.22, 0.18) * drawn
    return jnp.clip(drawn, min=-limit, max=limit).astype(kind)


def setup_inputs(seed: int = 0) -> dict:
    seeds = jax.random.split(jax.random.key(seed), 12)
    return {
        "residual": normal_values(seeds[0], (LENGTH_NODES, ACROSS_NODES, DEPTH_NODES), 1.0, 6.0, ((0, 4), (1, 2), (2, 4)), jnp.float32),
        "solution": normal_values(seeds[1], (LENGTH_NODES, ACROSS_NODES, DEPTH_NODES), 1.0, 6.0, ((0, 4), (1, 2), (2, 4)), jnp.float32),
        "direction": normal_values(seeds[2], (LENGTH_NODES, ACROSS_NODES, DEPTH_NODES), 1.0, 6.0, ((0, 4), (1, 2), (2, 4)), jnp.float32),
        "conductance": jnp.clip(jnp.exp(math.log(3.0) - 2.3025851 * jax.random.uniform(seeds[3], (3, LENGTH_NODES, ACROSS_NODES, DEPTH_NODES), jnp.float32) ** shard_levels(seeds[3], (3, LENGTH_NODES, ACROSS_NODES, DEPTH_NODES), ((1, 4), (2, 2), (3, 4)), -0.2, 0.2)), 0.3, 3.0),
        "mass_term": jnp.clip(0.2 + 0.8 * jax.random.uniform(seeds[4], (LENGTH_NODES, ACROSS_NODES, DEPTH_NODES), jnp.float32) ** shard_levels(seeds[4], (LENGTH_NODES, ACROSS_NODES, DEPTH_NODES), ((0, 4), (1, 2), (2, 4)), -0.2, 0.2), 0.2, 1.0),
        "eigen_basis": normal_values(seeds[5], (ELEMENT_NODES + 2, ELEMENT_NODES + 2), (ELEMENT_NODES + 2) ** -0.5, 2.0, (), jnp.float32),
        "inverse_eigen_sums": jnp.clip(jnp.exp(math.log(1.0) - 2.3025851 * jax.random.uniform(seeds[6], ((ELEMENT_NODES + 2) * LENGTH_ELEMENTS, (ELEMENT_NODES + 2) * ACROSS_ELEMENTS, (ELEMENT_NODES + 2) * DEPTH_ELEMENTS), jnp.float32) ** shard_levels(seeds[6], ((ELEMENT_NODES + 2) * LENGTH_ELEMENTS, (ELEMENT_NODES + 2) * ACROSS_ELEMENTS, (ELEMENT_NODES + 2) * DEPTH_ELEMENTS), ((0, 4), (1, 2), (2, 4)), -0.2, 0.2)), 0.1, 1.0),
        "element_coarse_index": touch_ends(jax.random.randint(seeds[7], (LENGTH_ELEMENTS, ACROSS_ELEMENTS, DEPTH_ELEMENTS), 0, DEVICE_COARSE), jax.random.fold_in(seeds[7], 1), 0, DEVICE_COARSE - 1).astype(jnp.int32),
        "xxt_values": normal_values(seeds[8], (XB * DEVICES, DEVICE_COARSE, BS), (DEVICE_COARSE * 128) ** -0.5, 0.0625, ((0, 32),), jnp.float32),
        "xxt_blocks": touch_ends(jax.random.randint(seeds[9], (XB * DEVICES,), 0, NB), jax.random.fold_in(seeds[9], 1), 0, NB - 1).astype(jnp.int32),
        "prior_inner": jnp.clip(jnp.exp(jax.random.uniform(seeds[10], (1,), jnp.float32, math.log(409600.0), math.log(1638400))), 409600.0, 1638400),
    }


HIGH = lax.Precision.HIGHEST


def cheb_matrix():
    count = 8
    points = np.cos(np.pi * np.arange(count) / (count - 1))
    signs = np.array([2.0, 1, 1, 1, 1, 1, 1, 2.0]) * (-1.0) ** np.arange(count)
    differ = points[:, None] - points[None, :] + np.eye(count)
    matrix = np.outer(signs, 1.0 / signs) / differ
    matrix = matrix - np.eye(count) * np.sum(matrix, axis=1)[:, None]
    return (0.25 * matrix).astype(np.float32)


def extended_index(count):
    parts = [np.array([8 * element] + list(range(8 * element + 2, 8 * element + 10)) + [8 * element + 11]) for element in range(count)]
    return np.concatenate(parts).astype(np.int32)


def inside_index(count):
    parts = [np.arange(10 * element + 1, 10 * element + 9) for element in range(count)]
    return np.concatenate(parts).astype(np.int32)


def assemble_padded(padded):
    result = padded
    for which_axis in range(3):
        length = result.shape[which_axis] - 2
        position = np.arange(length) % 8
        shape_list = [1, 1, 1]
        shape_list[which_axis] = length
        upper = jnp.asarray((position == 7).astype(np.float32).reshape(shape_list))
        lower = jnp.asarray((position == 0).astype(np.float32).reshape(shape_list))
        centre = lax.slice_in_dim(result, 1, length + 1, axis=which_axis)
        above = lax.slice_in_dim(result, 2, length + 2, axis=which_axis)
        below = lax.slice_in_dim(result, 0, length, axis=which_axis)
        result = centre + upper * above + lower * below
    return result


def along_axis(matrix, values, which_axis):
    moved = jnp.moveaxis(values, which_axis, -1)
    width_one = matrix.shape[1]
    blocks = moved.reshape(moved.shape[:-1] + (moved.shape[-1] // width_one, width_one))
    mapped = jnp.einsum('ij,...ej->...ei', matrix, blocks, precision=HIGH)
    return jnp.moveaxis(mapped.reshape(moved.shape), -1, which_axis)


def local_operator(values, conductance, mass_term, matrix):
    total = mass_term * values
    for which_axis in range(3):
        grad = along_axis(matrix, values, which_axis)
        total = total + along_axis(matrix.T, conductance[which_axis] * grad, which_axis)
    return total


def reference(residual, solution, direction, conductance, mass_term, eigen_basis, inverse_eigen_sums, element_coarse_index, xxt_values, xxt_blocks, prior_inner):
    matrix = jnp.asarray(cheb_matrix())
    devices_all = N_GX * N_GY * N_GZ
    padded = jnp.pad(residual, 2)
    extended_element = jnp.take(padded, jnp.asarray(extended_index(LENGTH_ELEMENTS)), axis=0)
    extended_element = jnp.take(extended_element, jnp.asarray(extended_index(ACROSS_ELEMENTS)), axis=1)
    extended_element = jnp.take(extended_element, jnp.asarray(extended_index(DEPTH_ELEMENTS)), axis=2)
    spectral = extended_element
    for which_axis in range(3):
        spectral = along_axis(eigen_basis.T, spectral, which_axis)
    spectral = inverse_eigen_sums * spectral
    for which_axis in range(3):
        spectral = along_axis(eigen_basis, spectral, which_axis)
    local_solution = spectral
    device_portion = jnp.take(local_solution, jnp.asarray(inside_index(LENGTH_ELEMENTS)), axis=0)
    device_portion = jnp.take(device_portion, jnp.asarray(inside_index(ACROSS_ELEMENTS)), axis=1)
    device_portion = jnp.take(device_portion, jnp.asarray(inside_index(DEPTH_ELEMENTS)), axis=2)
    element_sum = residual.reshape(LENGTH_ELEMENTS, 8, ACROSS_ELEMENTS, 8, DEPTH_ELEMENTS, 8).sum(axis=(1, 3, 5))
    dev_x = (jnp.arange(LENGTH_ELEMENTS) // EX).astype(jnp.int32)
    dev_y = (jnp.arange(ACROSS_ELEMENTS) // EY).astype(jnp.int32)
    device_depth = (jnp.arange(DEPTH_ELEMENTS) // DEVICE_DEPTH_ELS).astype(jnp.int32)
    owner = (dev_x[:, None, None] * N_GY + dev_y[None, :, None]) * N_GZ + device_depth[None, None, :]
    global_ids = (owner * DEVICE_COARSE + element_coarse_index).astype(jnp.int32)
    coarse_residual = jnp.zeros((NC,), jnp.float32).at[global_ids.ravel()].add(element_sum.ravel())
    values_four = xxt_values.reshape(devices_all, XB, DEVICE_COARSE, BS)
    contrib = jnp.einsum('dknb,dn->dkb', values_four, coarse_residual.reshape(devices_all, DEVICE_COARSE), precision=HIGH)
    coarse_inner = jnp.zeros((NB, BS), jnp.float32).at[xxt_blocks].add(contrib.reshape(devices_all * XB, BS))
    picked = coarse_inner[xxt_blocks].reshape(devices_all, XB, BS)
    coarse_solution = jnp.einsum('dknb,dkb->dn', values_four, picked, precision=HIGH).ravel()
    element_coarse = coarse_solution[global_ids]
    spread_values = jnp.broadcast_to(element_coarse[:, None, :, None, :, None], (LENGTH_ELEMENTS, 8, ACROSS_ELEMENTS, 8, DEPTH_ELEMENTS, 8)).reshape(LENGTH_NODES, ACROSS_NODES, DEPTH_NODES)
    preconditioned = device_portion + spread_values
    inner = jnp.sum(extended_element * local_solution) + jnp.sum(coarse_inner * coarse_inner)
    new_direction = preconditioned + (inner / prior_inner[0]) * direction
    image = local_operator(new_direction, conductance, mass_term, matrix)
    curvature = jnp.sum(new_direction * image)
    alpha = inner / curvature
    new_solution = solution + alpha * new_direction
    new_residual = residual - alpha * assemble_padded(jnp.pad(image, 1))
    return new_solution, new_residual, new_direction
```

```python
import functools

import jax
import jax.numpy as jnp
import numpy as np
from jax import lax
from jax.experimental import pallas as pl
from jax.experimental.pallas import tpu as pltpu
from jax.sharding import PartitionSpec as P

MESH = pl.DeviceIdType.MESH
HIGHEST = lax.Precision.HIGHEST
F32 = jnp.float32
BF16 = jnp.bfloat16


def cheb_matrix():
    count = 8
    points = np.cos(np.pi * np.arange(count) / (count - 1))
    signs = np.array([2.0, 1, 1, 1, 1, 1, 1, 2.0]) * (-1.0) ** np.arange(count)
    differ = points[:, None] - points[None, :] + np.eye(count)
    matrix = np.outer(signs, 1.0 / signs) / differ
    matrix = matrix - np.eye(count) * np.sum(matrix, axis=1)[:, None]
    return (0.25 * matrix).astype(np.float32)


NN = (((1,), (0,)), ((), ()))
NT = (((1,), (1,)), ((), ()))
TN = (((0,), (0,)), ((), ()))


def split2(a):
    hi = a.astype(BF16)
    return hi, (a - hi.astype(F32)).astype(BF16)


def dot3(a, b, dims):
    ah, al = split2(a)
    bh, bl = b
    dot = lambda x, y: lax.dot_general(x, y, dims, preferred_element_type=F32)
    return dot(ah, bh) + (dot(ah, bl) + dot(al, bh))


def exact_dot(a, b, dims):
    return lax.dot_general(a, b, dims, precision=HIGHEST, preferred_element_type=F32)


def iota(shape, axis):
    return lax.broadcasted_iota(jnp.int32, shape, axis)


def group_stages(nx, ny, nz):
    if ny * nz <= 8:
        first = [(0, b, c) for b in range(ny) for c in range(nz) if (b, c) != (0, 0)]
        stages = [first]
    else:
        stages = [[(0, 0, c) for c in range(1, nz)], [(0, b, 0) for b in range(1, ny)]]
    return stages + [[(a, 0, 0) for a in range(1, nx)]]


def node_rows(elem, count, low, high):
    rows = [8 * elem - 2] + list(range(8 * elem, 8 * elem + 8)) + [8 * elem + 9]
    return [low if r < 0 else high if r >= 8 * count else r for r in rows]


def kernel(
    sizes,
    stages,
    res, sol, dirn, cond, mass, eb_s, eb, inv, idx, xv, xb, prior, dmat, dz,
    nsol, nres, ndir,
    zs, zr, q, ys, yr, ts, inv2, ws, lp, part, aslot, cin,
    zs2, zr2, g2, ys2, xr2, yr2, sc, bslot,
    hs, hr, as_, ar, bs_, br,
):
    nx, ny, nz = sizes
    ix, iy, iz = lax.axis_index("gx"), lax.axis_index("gy"), lax.axis_index("gz")
    D = cheb_matrix()
    have = {
        ("x", -1): ix > 0, ("x", 1): ix < nx - 1,
        ("y", -1): iy > 0, ("y", 1): iy < ny - 1,
        ("z", -1): iz > 0, ("z", 1): iz < nz - 1,
    }

    barrier = pltpu.get_barrier_semaphore()
    all_offsets = [o for stage in stages for o in stage]

    def partner(o):
        return (lax.rem(ix + o[0], nx), lax.rem(iy + o[1], ny), lax.rem(iz + o[2], nz))

    corners = {(a % nx, b % ny, 0) for a in (-1, 1) for b in (-1, 1)} - set(all_offsets) - {(0, 0, 0)}
    greeted = all_offsets + sorted(corners)
    for o in greeted:
        pl.semaphore_signal(barrier, inc=1, device_id=partner(o), device_id_type=MESH)

    def message(k, src, dst, dev):
        return pltpu.make_async_remote_copy(
            src_ref=src, dst_ref=dst, send_sem=hs.at[k], recv_sem=hr.at[k],
            device_id=dev, device_id_type=MESH,
        )

    def start(items):
        for send_if, recv_if, args in items:
            @pl.when(send_if)
            def _(args=args):
                message(*args).start()

    def wait_recv(items):
        for send_if, recv_if, args in items:
            @pl.when(recv_if)
            def _(args=args):
                message(*args).wait_recv()

    def wait_send(items):
        for send_if, recv_if, args in items:
            @pl.when(send_if)
            def _(args=args):
                message(*args).wait_send()

    def z_items(base, src, dst):
        return [
            (have["z", 1], have["z", -1], (base, src.at[1], dst.at[0], (ix, iy, iz + 1))),
            (have["z", -1], have["z", 1], (base + 1, src.at[0], dst.at[1], (ix, iy, iz - 1))),
        ]

    def face_items(base, x_src, x_dst, y_src, y_dst, lead):
        items = []
        for n, s in ((0, 1), (1, -1)):
            low = 0 if s == 1 else 1
            items.append((have["x", s], have["x", -s], (base + n, x_src[s], x_dst[-s], (ix + s, iy, iz))))
            near = (low,) + lead + (pl.ds(0, 16),)
            items.append((have["y", s], have["y", -s],
                          (base + 2 + n, y_src.at[(1 - low,)], y_dst.at[near], (ix, iy + s, iz))))
        k = base + 4
        for a in (1, -1):
            for b in (1, -1):
                rows = pl.ds(8, 8) if a == 1 else pl.ds(0, 8)
                drows = pl.ds(16, 8) if a == 1 else pl.ds(24, 8)
                side, dside = (1, 0) if b == 1 else (0, 1)
                items.append((have["x", a] & have["y", b], have["x", -a] & have["y", -b],
                              (k, y_src.at[(side,) + lead + (rows,)], y_dst.at[(dside,) + lead + (drows,)],
                               (ix + a, iy + b, iz))))
                k += 1
        return items

    full = (slice(None),)
    z1 = z_items(0, zs, zr)
    f1 = face_items(2, {1: q.at[14, pl.ds(0, 16)], -1: q.at[1, pl.ds(0, 16)]},
                    {-1: q.at[16, pl.ds(0, 16)], 1: q.at[17, pl.ds(0, 16)]}, ys, yr, ())
    z2 = z_items(10, zs2, zr2)
    f2 = face_items(12, {1: g2.at[:, 15], -1: g2.at[:, 0]}, {-1: xr2.at[0], 1: xr2.at[1]}, ys2, yr2, full)

    def ring(stage_no, src, slots, ss, rs):
        base = sum(len(s) for s in stages[:stage_no])
        return [
            pltpu.make_async_remote_copy(
                src_ref=src.at[stage_no], dst_ref=slots.at[base + n],
                send_sem=ss.at[base + n], recv_sem=rs.at[base + n],
                device_id=partner(o), device_id_type=MESH,
            )
            for n, o in enumerate(stages[stage_no])
        ]

    def ring_sum(stage_no, src, slots, copies):
        base = sum(len(s) for s in stages[:stage_no])
        total = src[stage_no]
        for n, c in enumerate(copies):
            c.wait_recv()
            total = total + slots[base + n]
        return total

    zero_z = jnp.zeros(zr.shape[1:], F32)
    zero_z2 = jnp.zeros(zr2.shape[1:], F32)
    for s, slot in ((-1, 0), (1, 1)):
        @pl.when(jnp.logical_not(have["z", s]))
        def _(slot=slot):
            zr[slot] = zero_z
            zr2[slot] = zero_z2

        @pl.when(jnp.logical_not(have["x", s]))
        def _(slot=slot):
            q[16 + slot, 0:16] = jnp.zeros((16, q.shape[2]), F32)
            xr2[slot] = jnp.zeros(xr2.shape[1:], F32)

        @pl.when(jnp.logical_not(have["y", s]))
        def _(slot=slot):
            yr[slot, 0:16] = jnp.zeros((16, yr.shape[2]), F32)
            yr2[slot, :, 0:16] = jnp.zeros((2, 16, yr2.shape[3]), F32)
    for a in (-1, 1):
        for b in (-1, 1):
            @pl.when(jnp.logical_not(have["x", a] & have["y", b]))
            def _(a=a, b=b):
                r = 16 if a == -1 else 24
                slot = 0 if b == -1 else 1
                yr[slot, r:r + 8] = jnp.zeros((8, yr.shape[2]), F32)
                yr2[slot, :, r:r + 8] = jnp.zeros((2, 8, yr2.shape[3]), F32)

    lanes = res.shape[2]
    wide = q.shape[2]
    r2d = res[...].reshape(256, lanes)
    rt = jnp.transpose(r2d)
    zs[0] = rt[0:8]
    zs[1] = rt[lanes - 8:lanes]

    elem_z = lanes // 8
    expand = (iota((elem_z, lanes), 1) // 8 == iota((elem_z, lanes), 0)).astype(BF16)
    coarse = xv.shape[1]
    masks = []
    acc = jnp.zeros((coarse, lanes), F32)
    for ex in range(2):
        for ey in range(2):
            ids = idx[ex, ey:ey + 1, :].astype(F32).astype(BF16)
            spread_ids = lax.dot_general(ids, expand, NN, preferred_element_type=F32)
            mask = spread_ids == iota((coarse, lanes), 0).astype(F32)
            masks.append(mask)
            block = res[8 * ex:8 * ex + 8, 8 * ey:8 * ey + 8, :]
            colsum = jnp.sum(jnp.sum(block, axis=0), axis=0, keepdims=True)
            acc = acc + jnp.where(mask, colsum, 0.0)
    coarse_res = jnp.sum(acc, axis=1, keepdims=True)
    nb = part.shape[1]
    partial = jnp.zeros((nb, xv.shape[2]), F32)
    rows_b = iota((nb, xv.shape[2]), 0)
    for k in range(xv.shape[0]):
        contrib = jnp.sum(xv[k] * coarse_res, axis=0, keepdims=True)
        partial = partial + jnp.where(rows_b == xb[k], contrib, 0.0)
    part[0] = partial

    pl.semaphore_wait(barrier, len(greeted))
    start(z1)
    a_copies = [ring(0, part, aslot, as_, ar)]
    for c in a_copies[0]:
        c.start()

    cols = iota((1, wide), 1)
    elem_of = sum((cols >= 10 * k).astype(jnp.int32) for k in range(1, elem_z))
    pick = (iota((10, wide), 0) == cols - 10 * elem_of).astype(F32)
    bwide = exact_dot(eb[...], pick, NN)
    dist = iota((lanes, wide), 0) - 8 * elem_of
    inner_part = jnp.zeros((lanes, wide), F32)
    for i in range(1, 9):
        inner_part = jnp.where(dist == i - 1, bwide[i:i + 1], inner_part)
    zfwd = jnp.where(dist == -2, bwide[0:1], jnp.where(dist == 9, bwide[9:10], inner_part))
    zfwd = split2(zfwd)
    zinv = split2(inner_part)
    rows16 = iota((16, wide), 0)
    zhalo = jnp.where((rows16 == 6) & (cols < 10), bwide[0:1], 0.0)
    zhalo = jnp.where((rows16 == 9) & (cols >= wide - 10), bwide[9:10], zhalo)
    zhalo = split2(zhalo)
    ebt = exact_dot((iota((16, 10), 0) == iota((16, 10), 1)).astype(F32), eb[...], NT)

    own = dot3(r2d, zfwd, NN)
    inv2[...] = jnp.zeros(inv2.shape, F32)
    for ey in range(2):
        inv2[:, ey, 0:10, :] = inv[:, 10 * ey:10 * ey + 10, :]

    wait_recv(z1)
    halo = jnp.concatenate([zr[0], zr[1]], axis=0)
    qv = (own + dot3(jnp.transpose(halo), zhalo, NN)).reshape(16, 16, wide)
    q[0:16, 0:16, :] = qv
    ys[0] = qv[:, 1, :]
    ys[1] = qv[:, 14, :]
    start(f1)

    dzs = split2(dz[...])

    def local_op(v):
        v4 = v.reshape(2, 8, 16, lanes)
        planes = [v4[:, j] for j in range(8)]
        cg = []
        for a in range(8):
            g = planes[0] * float(D[a, 0])
            for j in range(1, 8):
                g = g + planes[j] * float(D[a, j])
            cg.append(g * cond[0].reshape(2, 8, 16, lanes)[:, a])
        outs = []
        for i in range(8):
            o = cg[0] * float(D[0, i])
            for a in range(1, 8):
                o = o + cg[a] * float(D[a, i])
            outs.append(o)
        total = jnp.stack(outs, axis=1).reshape(16, 16, lanes) + mass[...] * v
        vy = v.reshape(16, 2, 8, lanes)
        g = vy[:, :, 0:1, :] * dmat[:, 0:1]
        for j in range(1, 8):
            g = g + vy[:, :, j:j + 1, :] * dmat[:, j:j + 1]
        g = g * cond[1].reshape(16, 2, 8, lanes)
        o = g[:, :, 0:1, :] * dmat[:, 8:9]
        for j in range(1, 8):
            o = o + g[:, :, j:j + 1, :] * dmat[:, 8 + j:9 + j]
        total = total + o.reshape(16, 16, lanes)
        gz = dot3(v.reshape(256, lanes), dzs, NT) * cond[2].reshape(256, lanes)
        return total + dot3(gz, dzs, NN).reshape(16, 16, lanes)

    dv = dirn[...]
    ld = local_op(dv)
    g2[1] = ld
    ldt = jnp.transpose(ld.reshape(256, lanes))
    zs2[0, 1] = ldt[0:8]
    zs2[1, 1] = ldt[lanes - 8:lanes]
    sc[0] = jnp.zeros((8, lanes), F32)
    sc[0, 2:3, :] = jnp.sum(jnp.sum(dv * ld, axis=0), axis=0, keepdims=True)

    for st in range(1, len(stages)):
        part[st] = ring_sum(st - 1, part, aslot, a_copies[st - 1])
        a_copies.append(ring(st, part, aslot, as_, ar))
        for c in a_copies[st]:
            c.start()

    wait_recv(f1)
    for s in range(2):
        q[0:16, 16 + s:17 + s, :] = yr[s, 0:16].reshape(16, 1, wide)
        q[16, 16 + s:17 + s, :] = yr[s, 22:23]
        q[17, 16 + s:17 + s, :] = yr[s, 25:26]
    for ey in range(2):
        t = None
        for j, row in enumerate(node_rows(ey, 2, 16, 17)):
            term = q[:, row:row + 1, :] * ebt[:, j:j + 1]
            t = term if t is None else t + term
        ts[:, ey] = t
    maps = [node_rows(ex, 2, 16, 17) for ex in range(2)]
    planes = [jnp.stack([ts[maps[0][i]], ts[maps[1][i]]]) for i in range(10)]
    inner_acc = None
    for a in range(10):
        u = planes[0] * eb_s[0, a]
        for i in range(1, 10):
            u = u + planes[i] * eb_s[i, a]
        w = u * jnp.stack([inv2[a], inv2[10 + a]])
        ws[a] = w
        term = u * w
        inner_acc = term if inner_acc is None else inner_acc + term
    inner_row = jnp.sum(jnp.sum(inner_acc, axis=(0, 1)), axis=0, keepdims=True)
    inner_local = jnp.sum(inner_row, axis=1, keepdims=True)
    sc[0, 3:4, :] = jnp.where(iota((1, lanes), 1) == 0, inner_local, 0.0)

    back = dot3(ws[...].reshape(640, wide), zinv, NT).reshape(10, 2, 2, 16, lanes)
    for m in range(8):
        o = back[0] * eb_s[m + 1, 0]
        for a in range(1, 10):
            o = o + back[a] * eb_s[m + 1, a]
        y = None
        for a in range(10):
            term = o[:, :, a:a + 1, :] * eb[1:9, a:a + 1]
            y = term if y is None else y + term
        lp[:, m] = y

    last = len(stages) - 1
    coarse_inner = ring_sum(last, part, aslot, a_copies[last])
    cin[...] = coarse_inner
    coarse_square = jnp.sum(jnp.sum(coarse_inner * coarse_inner, axis=0, keepdims=True), axis=1, keepdims=True)
    acc = None
    for k in range(xv.shape[0]):
        term = xv[k] * cin[pl.ds(xb[k], 1), :]
        acc = term if acc is None else acc + term
    coarse_sol = jnp.sum(acc, axis=1, keepdims=True)
    for ex in range(2):
        for ey in range(2):
            row = jnp.sum(jnp.where(masks[2 * ex + ey], coarse_sol, 0.0), axis=0, keepdims=True)
            lp[ex, :, ey] = lp[ex, :, ey] + row
    z = lp[...].reshape(16, 16, lanes)
    lz = local_op(z)
    lzt = jnp.transpose(lz.reshape(256, lanes))
    zs2[0, 0] = lzt[0:8]
    zs2[1, 0] = lzt[lanes - 8:lanes]
    start(z2)
    g2[0] = lz
    sc[0, 0:1, :] = jnp.sum(jnp.sum(z * lz, axis=0), axis=0, keepdims=True)
    sc[0, 1:2, :] = jnp.sum(jnp.sum(z * g2[1], axis=0), axis=0, keepdims=True)
    b_copies = [ring(0, sc, bslot, bs_, br)]
    for c in b_copies[0]:
        c.start()

    lane = iota((256, lanes), 1)
    up = (lane % 8 == 7) & (lane < lanes - 1)
    down = (lane % 8 == 0) & (lane > 0)
    r16 = iota((16, lanes), 0)
    l16 = iota((16, lanes), 1)
    put = (((r16 == 7) & (l16 == 0)) | ((r16 == 8) & (l16 == lanes - 1))).astype(F32)
    inside = []
    for n in range(2):
        v = g2[n].reshape(256, lanes)
        inside.append(v + jnp.where(up, pltpu.roll(v, lanes - 1, 1), 0.0) + jnp.where(down, pltpu.roll(v, 1, 1), 0.0))
    wait_recv(z2)
    for n in range(2):
        halo = jnp.concatenate([zr2[0, n], zr2[1, n]], axis=0)
        v = (inside[n] + exact_dot(jnp.transpose(halo), put, NN)).reshape(16, 16, lanes)
        g2[n] = v
        ys2[0, n] = v[:, 0, :]
        ys2[1, n] = v[:, 15, :]
    start(f2)
    for st in range(1, len(stages)):
        sc[st] = ring_sum(st - 1, sc, bslot, b_copies[st - 1])
        b_copies.append(ring(st, sc, bslot, bs_, br))
        for c in b_copies[st]:
            c.start()

    wait_recv(f2)
    sub = iota((16, lanes), 0)
    assembled = []
    for n in range(2):
        def along_y(v, low, high):
            return v + jnp.where(sub == 0, low, jnp.where(sub == 7, v[:, 8:9, :], jnp.where(
                sub == 8, v[:, 7:8, :], jnp.where(sub == 15, high, 0.0))))
        v = along_y(g2[n], yr2[0, n, 0:16].reshape(16, 1, lanes), yr2[1, n, 0:16].reshape(16, 1, lanes))
        xlo = along_y(xr2[0, n:n + 1], yr2[0, n, 23:24].reshape(1, 1, lanes), yr2[1, n, 23:24].reshape(1, 1, lanes))
        xhi = along_y(xr2[1, n:n + 1], yr2[0, n, 24:25].reshape(1, 1, lanes), yr2[1, n, 24:25].reshape(1, 1, lanes))
        assembled.append(jnp.concatenate([
            v[0:1] + xlo, v[1:7], v[7:8] + v[8:9], v[8:9] + v[7:8], v[9:15], v[15:16] + xhi], axis=0))

    total = ring_sum(last, sc, bslot, b_copies[last])
    sums = jnp.sum(total, axis=1, keepdims=True)
    inner = sums[3:4] + coarse_square
    ratio = inner / prior[0]
    curvature = sums[0:1] + 2.0 * ratio * sums[1:2] + ratio * ratio * sums[2:3]
    alpha = inner / curvature
    p = lp[...].reshape(16, 16, lanes) + ratio.reshape(1, 1, 1) * dirn[...]
    ndir[...] = p
    nsol[...] = sol[...] + alpha.reshape(1, 1, 1) * p
    nres[...] = res[...] - alpha.reshape(1, 1, 1) * (assembled[0] + ratio.reshape(1, 1, 1) * assembled[1])

    wait_send(z1 + f1 + z2 + f2)
    for copies in a_copies + b_copies:
        for c in copies:
            c.wait_send()


def body(sizes, residual, solution, direction, conductance, mass_term, eigen_basis, inverse_eigen_sums,
         element_coarse_index, xxt_values, xxt_blocks, prior_inner):
    stages = group_stages(*sizes)
    sends = sum(len(s) for s in stages)
    lanes = residual.shape[2]
    wide = inverse_eigen_sums.shape[2]
    coarse = xxt_values.shape[1]
    bs = xxt_values.shape[2]
    nb = coarse * sizes[0] * sizes[1] * sizes[2] // bs
    base = cheb_matrix()
    dmat = jnp.asarray(np.concatenate([base, base.T], axis=1))
    dz = jnp.asarray(np.kron(np.eye(lanes // 8, dtype=np.float32), base))
    vmem = pl.BlockSpec(memory_space=pltpu.VMEM)
    smem = pl.BlockSpec(memory_space=pltpu.SMEM)
    out = jax.ShapeDtypeStruct(residual.shape, F32)
    ns = len(stages)
    return pl.pallas_call(
        functools.partial(kernel, sizes, stages),
        out_shape=(out, out, out),
        in_specs=[vmem, vmem, vmem, vmem, vmem, smem, vmem, vmem, vmem, vmem, smem, smem, vmem, vmem],
        out_specs=(vmem, vmem, vmem),
        scratch_shapes=[
            pltpu.VMEM((2, 8, 256), F32),
            pltpu.VMEM((2, 8, 256), F32),
            pltpu.VMEM((18, 24, wide), F32),
            pltpu.VMEM((2, 16, wide), F32),
            pltpu.VMEM((2, 32, wide), F32),
            pltpu.VMEM((18, 2, 16, wide), F32),
            pltpu.VMEM((20, 2, 16, wide), F32),
            pltpu.VMEM((10, 2, 2, 16, wide), F32),
            pltpu.VMEM((2, 8, 2, 8, lanes), F32),
            pltpu.VMEM((ns, nb, bs), F32),
            pltpu.VMEM((sends, nb, bs), F32),
            pltpu.VMEM((nb, bs), F32),
            pltpu.VMEM((2, 2, 8, 256), F32),
            pltpu.VMEM((2, 2, 8, 256), F32),
            pltpu.VMEM((2, 16, 16, lanes), F32),
            pltpu.VMEM((2, 2, 16, lanes), F32),
            pltpu.VMEM((2, 2, 16, lanes), F32),
            pltpu.VMEM((2, 2, 32, lanes), F32),
            pltpu.VMEM((ns, 8, lanes), F32),
            pltpu.VMEM((sends, 8, lanes), F32),
            pltpu.SemaphoreType.DMA((20,)),
            pltpu.SemaphoreType.DMA((20,)),
            pltpu.SemaphoreType.DMA((sends,)),
            pltpu.SemaphoreType.DMA((sends,)),
            pltpu.SemaphoreType.DMA((sends,)),
            pltpu.SemaphoreType.DMA((sends,)),
        ],
        compiler_params=pltpu.CompilerParams(
            collective_id=0, has_side_effects=True, vmem_limit_bytes=48 * 1024 * 1024
        ),
    )(residual, solution, direction, conductance, mass_term, eigen_basis, eigen_basis, inverse_eigen_sums,
      element_coarse_index, xxt_values, xxt_blocks, prior_inner, dmat, dz)


def solution(mesh):
    grid = P("gx", "gy", "gz")
    in_specs = (
        grid, grid, grid, P(None, "gx", "gy", "gz"), grid, P(), grid, grid,
        P(("gx", "gy", "gz"), None, None), P(("gx", "gy", "gz")), P(),
    )
    sizes = (mesh.shape["gx"], mesh.shape["gy"], mesh.shape["gz"])
    return jax.shard_map(functools.partial(body, sizes), mesh=mesh, in_specs=in_specs,
                         out_specs=(grid, grid, grid), check_vma=False)
```

```python
import functools

import jax
import jax.numpy as jnp
import numpy as np
from jax import lax
from jax.experimental import pallas as pl
from jax.experimental.pallas import tpu as pltpu
from jax.sharding import PartitionSpec as P

MESH = pl.DeviceIdType.MESH
HIGHEST = lax.Precision.HIGHEST
F32 = jnp.float32
BF16 = jnp.bfloat16


def cheb_matrix():
    count = 8
    points = np.cos(np.pi * np.arange(count) / (count - 1))
    signs = np.array([2.0, 1, 1, 1, 1, 1, 1, 2.0]) * (-1.0) ** np.arange(count)
    differ = points[:, None] - points[None, :] + np.eye(count)
    matrix = np.outer(signs, 1.0 / signs) / differ
    matrix = matrix - np.eye(count) * np.sum(matrix, axis=1)[:, None]
    return (0.25 * matrix).astype(np.float32)


NN = (((1,), (0,)), ((), ()))
NT = (((1,), (1,)), ((), ()))
TN = (((0,), (0,)), ((), ()))


def split2(a):
    hi = a.astype(BF16)
    return hi, (a - hi.astype(F32)).astype(BF16)


def dot3(a, b, dims):
    ah, al = split2(a)
    bh, bl = b
    dot = lambda x, y: lax.dot_general(x, y, dims, preferred_element_type=F32)
    return dot(ah, bh) + (dot(ah, bl) + dot(al, bh))


def exact_dot(a, b, dims):
    return lax.dot_general(a, b, dims, precision=HIGHEST, preferred_element_type=F32)


def iota(shape, axis):
    return lax.broadcasted_iota(jnp.int32, shape, axis)


def group_stages(nx, ny, nz):
    if ny * nz <= 8:
        first = [(0, b, c) for b in range(ny) for c in range(nz) if (b, c) != (0, 0)]
        stages = [first]
    else:
        stages = [[(0, 0, c) for c in range(1, nz)], [(0, b, 0) for b in range(1, ny)]]
    return stages + [[(a, 0, 0) for a in range(1, nx)]]


def node_rows(elem, count, low, high):
    rows = [8 * elem - 2] + list(range(8 * elem, 8 * elem + 8)) + [8 * elem + 9]
    return [low if r < 0 else high if r >= 8 * count else r for r in rows]


def kernel(
    sizes,
    stages,
    h_res, h_sol, h_dirn, h_cond, h_mass, h_eb, h_inv, h_idx, h_xv, h_xb, h_prior, h_dmat, h_dz,
    o_sol, o_res, o_dir,
    res, sol, dirn, cond, mass, eb, inv, idx, xv, xb, prior, dmat, dz, eb_s,
    zs, zr, q, ys, yr, ts, inv2, ws, lp, part, aslot, cin,
    zs2, zr2, g2, ys2, xr2, yr2, sc, bslot,
    nsol, nres, ndir, hs, hr, as_, ar, bs_, br, ls, os_,
):
    nx, ny, nz = sizes
    ix, iy, iz = lax.axis_index("gx"), lax.axis_index("gy"), lax.axis_index("gz")
    D = cheb_matrix()
    have = {
        ("x", -1): ix > 0, ("x", 1): ix < nx - 1,
        ("y", -1): iy > 0, ("y", 1): iy < ny - 1,
        ("z", -1): iz > 0, ("z", 1): iz < nz - 1,
    }

    pairs = dict(
        res=(h_res, res), eb=(h_eb, eb), eb_s=(h_eb, eb_s), xv=(h_xv, xv), idx=(h_idx, idx), xb=(h_xb, xb),
        dirn=(h_dirn, dirn), cond=(h_cond, cond), mass=(h_mass, mass), dmat=(h_dmat, dmat), dz=(h_dz, dz),
        inv=(h_inv, inv), sol=(h_sol, sol), prior=(h_prior, prior),
    )
    loads = {name: pltpu.make_async_copy(src, dst, ls.at[n]) for n, (name, (src, dst)) in enumerate(pairs.items())}

    def arrived(*names):
        for name in names:
            loads[name].wait()

    barrier = pltpu.get_barrier_semaphore()
    all_offsets = [o for stage in stages for o in stage]

    def partner(o):
        return (lax.rem(ix + o[0], nx), lax.rem(iy + o[1], ny), lax.rem(iz + o[2], nz))

    corners = {(a % nx, b % ny, 0) for a in (-1, 1) for b in (-1, 1)} - set(all_offsets) - {(0, 0, 0)}
    greeted = all_offsets + sorted(corners)
    for o in greeted:
        pl.semaphore_signal(barrier, inc=1, device_id=partner(o), device_id_type=MESH)

    for copy in loads.values():
        copy.start()

    def message(k, src, dst, dev):
        return pltpu.make_async_remote_copy(
            src_ref=src, dst_ref=dst, send_sem=hs.at[k], recv_sem=hr.at[k],
            device_id=dev, device_id_type=MESH,
        )

    def start(items):
        for send_if, recv_if, args in items:
            @pl.when(send_if)
            def _(args=args):
                message(*args).start()

    def wait_recv(items):
        for send_if, recv_if, args in items:
            @pl.when(recv_if)
            def _(args=args):
                message(*args).wait_recv()

    def wait_send(items):
        for send_if, recv_if, args in items:
            @pl.when(send_if)
            def _(args=args):
                message(*args).wait_send()

    def z_items(base, src, dst):
        return [
            (have["z", 1], have["z", -1], (base, src.at[1], dst.at[0], (ix, iy, iz + 1))),
            (have["z", -1], have["z", 1], (base + 1, src.at[0], dst.at[1], (ix, iy, iz - 1))),
        ]

    def face_items(base, x_src, x_dst, y_src, y_dst, lead):
        items = []
        for n, s in ((0, 1), (1, -1)):
            low = 0 if s == 1 else 1
            items.append((have["x", s], have["x", -s], (base + n, x_src[s], x_dst[-s], (ix + s, iy, iz))))
            near = (low,) + lead + (pl.ds(0, 16),)
            items.append((have["y", s], have["y", -s],
                          (base + 2 + n, y_src.at[(1 - low,)], y_dst.at[near], (ix, iy + s, iz))))
        k = base + 4
        for a in (1, -1):
            for b in (1, -1):
                rows = pl.ds(8, 8) if a == 1 else pl.ds(0, 8)
                drows = pl.ds(16, 8) if a == 1 else pl.ds(24, 8)
                side, dside = (1, 0) if b == 1 else (0, 1)
                items.append((have["x", a] & have["y", b], have["x", -a] & have["y", -b],
                              (k, y_src.at[(side,) + lead + (rows,)], y_dst.at[(dside,) + lead + (drows,)],
                               (ix + a, iy + b, iz))))
                k += 1
        return items

    full = (slice(None),)
    z1 = z_items(0, zs, zr)
    f1 = face_items(2, {1: q.at[14, pl.ds(0, 16)], -1: q.at[1, pl.ds(0, 16)]},
                    {-1: q.at[16, pl.ds(0, 16)], 1: q.at[17, pl.ds(0, 16)]}, ys, yr, ())
    z2 = z_items(10, zs2, zr2)
    f2 = face_items(12, {1: g2.at[:, 15], -1: g2.at[:, 0]}, {-1: xr2.at[0], 1: xr2.at[1]}, ys2, yr2, full)

    def ring(stage_no, src, slots, ss, rs):
        base = sum(len(s) for s in stages[:stage_no])
        return [
            pltpu.make_async_remote_copy(
                src_ref=src.at[stage_no], dst_ref=slots.at[base + n],
                send_sem=ss.at[base + n], recv_sem=rs.at[base + n],
                device_id=partner(o), device_id_type=MESH,
            )
            for n, o in enumerate(stages[stage_no])
        ]

    def ring_sum(stage_no, src, slots, copies):
        base = sum(len(s) for s in stages[:stage_no])
        total = src[stage_no]
        for n, c in enumerate(copies):
            c.wait_recv()
            total = total + slots[base + n]
        return total

    zero_z = jnp.zeros(zr.shape[1:], F32)
    zero_z2 = jnp.zeros(zr2.shape[1:], F32)
    for s, slot in ((-1, 0), (1, 1)):
        @pl.when(jnp.logical_not(have["z", s]))
        def _(slot=slot):
            zr[slot] = zero_z
            zr2[slot] = zero_z2

        @pl.when(jnp.logical_not(have["x", s]))
        def _(slot=slot):
            q[16 + slot, 0:16] = jnp.zeros((16, q.shape[2]), F32)
            xr2[slot] = jnp.zeros(xr2.shape[1:], F32)

        @pl.when(jnp.logical_not(have["y", s]))
        def _(slot=slot):
            yr[slot, 0:16] = jnp.zeros((16, yr.shape[2]), F32)
            yr2[slot, :, 0:16] = jnp.zeros((2, 16, yr2.shape[3]), F32)
    for a in (-1, 1):
        for b in (-1, 1):
            @pl.when(jnp.logical_not(have["x", a] & have["y", b]))
            def _(a=a, b=b):
                r = 16 if a == -1 else 24
                slot = 0 if b == -1 else 1
                yr[slot, r:r + 8] = jnp.zeros((8, yr.shape[2]), F32)
                yr2[slot, :, r:r + 8] = jnp.zeros((2, 8, yr2.shape[3]), F32)

    lanes = res.shape[2]
    wide = q.shape[2]
    elem_z = lanes // 8
    arrived("eb")
    cols = iota((1, wide), 1)
    elem_of = sum((cols >= 10 * k).astype(jnp.int32) for k in range(1, elem_z))
    pick = (iota((10, wide), 0) == cols - 10 * elem_of).astype(F32)
    bwide = exact_dot(eb[...], pick, NN)
    dist = iota((lanes, wide), 0) - 8 * elem_of
    inner_part = jnp.zeros((lanes, wide), F32)
    for i in range(1, 9):
        inner_part = jnp.where(dist == i - 1, bwide[i:i + 1], inner_part)
    zfwd = jnp.where(dist == -2, bwide[0:1], jnp.where(dist == 9, bwide[9:10], inner_part))
    zfwd = split2(zfwd)
    zinv = split2(inner_part)
    rows16 = iota((16, wide), 0)
    zhalo = jnp.where((rows16 == 6) & (cols < 10), bwide[0:1], 0.0)
    zhalo = jnp.where((rows16 == 9) & (cols >= wide - 10), bwide[9:10], zhalo)
    zhalo = split2(zhalo)
    ebt = exact_dot((iota((16, 10), 0) == iota((16, 10), 1)).astype(F32), eb[...], NT)

    arrived("res")
    r2d = res[...].reshape(256, lanes)
    rt = jnp.transpose(r2d)
    zs[0] = rt[0:8]
    zs[1] = rt[lanes - 8:lanes]

    arrived("idx", "xv", "xb")
    expand = (iota((elem_z, lanes), 1) // 8 == iota((elem_z, lanes), 0)).astype(BF16)
    coarse = xv.shape[1]
    masks = []
    acc = jnp.zeros((coarse, lanes), F32)
    for ex in range(2):
        for ey in range(2):
            ids = idx[ex, ey:ey + 1, :].astype(F32).astype(BF16)
            spread_ids = lax.dot_general(ids, expand, NN, preferred_element_type=F32)
            mask = spread_ids == iota((coarse, lanes), 0).astype(F32)
            masks.append(mask)
            block = res[8 * ex:8 * ex + 8, 8 * ey:8 * ey + 8, :]
            colsum = jnp.sum(jnp.sum(block, axis=0), axis=0, keepdims=True)
            acc = acc + jnp.where(mask, colsum, 0.0)
    coarse_res = jnp.sum(acc, axis=1, keepdims=True)
    nb = part.shape[1]
    partial = jnp.zeros((nb, xv.shape[2]), F32)
    rows_b = iota((nb, xv.shape[2]), 0)
    for k in range(xv.shape[0]):
        contrib = jnp.sum(xv[k] * coarse_res, axis=0, keepdims=True)
        partial = partial + jnp.where(rows_b == xb[k], contrib, 0.0)
    part[0] = partial

    pl.semaphore_wait(barrier, len(greeted))
    start(z1)
    a_copies = [ring(0, part, aslot, as_, ar)]
    for c in a_copies[0]:
        c.start()

    own = dot3(r2d, zfwd, NN)
    arrived("inv")
    inv2[...] = jnp.zeros(inv2.shape, F32)
    for ey in range(2):
        inv2[:, ey, 0:10, :] = inv[:, 10 * ey:10 * ey + 10, :]

    wait_recv(z1)
    halo = jnp.concatenate([zr[0], zr[1]], axis=0)
    qv = (own + dot3(jnp.transpose(halo), zhalo, NN)).reshape(16, 16, wide)
    q[0:16, 0:16, :] = qv
    ys[0] = qv[:, 1, :]
    ys[1] = qv[:, 14, :]
    start(f1)

    arrived("dz", "dirn", "cond", "mass", "dmat")
    dzs = split2(dz[...])

    def local_op(v):
        v4 = v.reshape(2, 8, 16, lanes)
        planes = [v4[:, j] for j in range(8)]
        cg = []
        for a in range(8):
            g = planes[0] * float(D[a, 0])
            for j in range(1, 8):
                g = g + planes[j] * float(D[a, j])
            cg.append(g * cond[0].reshape(2, 8, 16, lanes)[:, a])
        outs = []
        for i in range(8):
            o = cg[0] * float(D[0, i])
            for a in range(1, 8):
                o = o + cg[a] * float(D[a, i])
            outs.append(o)
        total = jnp.stack(outs, axis=1).reshape(16, 16, lanes) + mass[...] * v
        vy = v.reshape(16, 2, 8, lanes)
        g = vy[:, :, 0:1, :] * dmat[:, 0:1]
        for j in range(1, 8):
            g = g + vy[:, :, j:j + 1, :] * dmat[:, j:j + 1]
        g = g * cond[1].reshape(16, 2, 8, lanes)
        o = g[:, :, 0:1, :] * dmat[:, 8:9]
        for j in range(1, 8):
            o = o + g[:, :, j:j + 1, :] * dmat[:, 8 + j:9 + j]
        total = total + o.reshape(16, 16, lanes)
        gz = dot3(v.reshape(256, lanes), dzs, NT) * cond[2].reshape(256, lanes)
        return total + dot3(gz, dzs, NN).reshape(16, 16, lanes)

    dv = dirn[...]
    ld = local_op(dv)
    g2[1] = ld
    ldt = jnp.transpose(ld.reshape(256, lanes))
    zs2[0, 1] = ldt[0:8]
    zs2[1, 1] = ldt[lanes - 8:lanes]
    sc[0] = jnp.zeros((8, lanes), F32)
    sc[0, 2:3, :] = jnp.sum(jnp.sum(dv * ld, axis=0), axis=0, keepdims=True)

    for st in range(1, len(stages)):
        part[st] = ring_sum(st - 1, part, aslot, a_copies[st - 1])
        a_copies.append(ring(st, part, aslot, as_, ar))
        for c in a_copies[st]:
            c.start()

    arrived("eb_s", "sol", "prior")
    wait_recv(f1)
    for s in range(2):
        q[0:16, 16 + s:17 + s, :] = yr[s, 0:16].reshape(16, 1, wide)
        q[16, 16 + s:17 + s, :] = yr[s, 22:23]
        q[17, 16 + s:17 + s, :] = yr[s, 25:26]
    for ey in range(2):
        t = None
        for j, row in enumerate(node_rows(ey, 2, 16, 17)):
            term = q[:, row:row + 1, :] * ebt[:, j:j + 1]
            t = term if t is None else t + term
        ts[:, ey] = t
    maps = [node_rows(ex, 2, 16, 17) for ex in range(2)]
    planes = [jnp.stack([ts[maps[0][i]], ts[maps[1][i]]]) for i in range(10)]
    inner_acc = None
    for a in range(10):
        u = planes[0] * eb_s[0, a]
        for i in range(1, 10):
            u = u + planes[i] * eb_s[i, a]
        w = u * jnp.stack([inv2[a], inv2[10 + a]])
        ws[a] = w
        term = u * w
        inner_acc = term if inner_acc is None else inner_acc + term
    inner_row = jnp.sum(jnp.sum(inner_acc, axis=(0, 1)), axis=0, keepdims=True)
    inner_local = jnp.sum(inner_row, axis=1, keepdims=True)
    sc[0, 3:4, :] = jnp.where(iota((1, lanes), 1) == 0, inner_local, 0.0)

    back = dot3(ws[...].reshape(640, wide), zinv, NT).reshape(10, 2, 2, 16, lanes)
    for m in range(8):
        o = back[0] * eb_s[m + 1, 0]
        for a in range(1, 10):
            o = o + back[a] * eb_s[m + 1, a]
        y = None
        for a in range(10):
            term = o[:, :, a:a + 1, :] * eb[1:9, a:a + 1]
            y = term if y is None else y + term
        lp[:, m] = y

    last = len(stages) - 1
    coarse_inner = ring_sum(last, part, aslot, a_copies[last])
    cin[...] = coarse_inner
    coarse_square = jnp.sum(jnp.sum(coarse_inner * coarse_inner, axis=0, keepdims=True), axis=1, keepdims=True)
    acc = None
    for k in range(xv.shape[0]):
        term = xv[k] * cin[pl.ds(xb[k], 1), :]
        acc = term if acc is None else acc + term
    coarse_sol = jnp.sum(acc, axis=1, keepdims=True)
    for ex in range(2):
        for ey in range(2):
            row = jnp.sum(jnp.where(masks[2 * ex + ey], coarse_sol, 0.0), axis=0, keepdims=True)
            lp[ex, :, ey] = lp[ex, :, ey] + row
    z = lp[...].reshape(16, 16, lanes)
    lz = local_op(z)
    lzt = jnp.transpose(lz.reshape(256, lanes))
    zs2[0, 0] = lzt[0:8]
    zs2[1, 0] = lzt[lanes - 8:lanes]
    start(z2)
    g2[0] = lz
    sc[0, 0:1, :] = jnp.sum(jnp.sum(z * lz, axis=0), axis=0, keepdims=True)
    sc[0, 1:2, :] = jnp.sum(jnp.sum(z * g2[1], axis=0), axis=0, keepdims=True)
    b_copies = [ring(0, sc, bslot, bs_, br)]
    for c in b_copies[0]:
        c.start()

    lane = iota((256, lanes), 1)
    up = (lane % 8 == 7) & (lane < lanes - 1)
    down = (lane % 8 == 0) & (lane > 0)
    r16 = iota((16, lanes), 0)
    l16 = iota((16, lanes), 1)
    put = (((r16 == 7) & (l16 == 0)) | ((r16 == 8) & (l16 == lanes - 1))).astype(F32)
    inside = []
    for n in range(2):
        v = g2[n].reshape(256, lanes)
        inside.append(v + jnp.where(up, pltpu.roll(v, lanes - 1, 1), 0.0) + jnp.where(down, pltpu.roll(v, 1, 1), 0.0))
    wait_recv(z2)
    for n in range(2):
        halo = jnp.concatenate([zr2[0, n], zr2[1, n]], axis=0)
        v = (inside[n] + exact_dot(jnp.transpose(halo), put, NN)).reshape(16, 16, lanes)
        g2[n] = v
        ys2[0, n] = v[:, 0, :]
        ys2[1, n] = v[:, 15, :]
    start(f2)
    for st in range(1, len(stages)):
        sc[st] = ring_sum(st - 1, sc, bslot, b_copies[st - 1])
        b_copies.append(ring(st, sc, bslot, bs_, br))
        for c in b_copies[st]:
            c.start()

    wait_recv(f2)
    sub = iota((16, lanes), 0)
    assembled = []
    for n in range(2):
        def along_y(v, low, high):
            return v + jnp.where(sub == 0, low, jnp.where(sub == 7, v[:, 8:9, :], jnp.where(
                sub == 8, v[:, 7:8, :], jnp.where(sub == 15, high, 0.0))))
        v = along_y(g2[n], yr2[0, n, 0:16].reshape(16, 1, lanes), yr2[1, n, 0:16].reshape(16, 1, lanes))
        xlo = along_y(xr2[0, n:n + 1], yr2[0, n, 23:24].reshape(1, 1, lanes), yr2[1, n, 23:24].reshape(1, 1, lanes))
        xhi = along_y(xr2[1, n:n + 1], yr2[0, n, 24:25].reshape(1, 1, lanes), yr2[1, n, 24:25].reshape(1, 1, lanes))
        assembled.append(jnp.concatenate([
            v[0:1] + xlo, v[1:7], v[7:8] + v[8:9], v[8:9] + v[7:8], v[9:15], v[15:16] + xhi], axis=0))

    total = ring_sum(last, sc, bslot, b_copies[last])
    sums = jnp.sum(total, axis=1, keepdims=True)
    inner = sums[3:4] + coarse_square
    ratio = inner / prior[0]
    curvature = sums[0:1] + 2.0 * ratio * sums[1:2] + ratio * ratio * sums[2:3]
    alpha = inner / curvature
    p = lp[...].reshape(16, 16, lanes) + ratio.reshape(1, 1, 1) * dirn[...]
    ndir[...] = p
    saves = [pltpu.make_async_copy(src, dst, os_.at[n]) for n, (src, dst) in enumerate(
        ((nsol, o_sol), (nres, o_res), (ndir, o_dir)))]
    saves[2].start()
    nsol[...] = sol[...] + alpha.reshape(1, 1, 1) * p
    saves[0].start()
    nres[...] = res[...] - alpha.reshape(1, 1, 1) * (assembled[0] + ratio.reshape(1, 1, 1) * assembled[1])

    saves[1].start()
    wait_send(z1 + f1 + z2 + f2)
    for copies in a_copies + b_copies:
        for c in copies:
            c.wait_send()
    for copy in saves:
        copy.wait()


def write_out(a, b, c, ao, bo, co, sems):
    copies = [pltpu.make_async_copy(src, dst, sems.at[n]) for n, (src, dst) in enumerate(((a, ao), (b, bo), (c, co)))]
    for copy in copies:
        copy.start()
    for copy in copies:
        copy.wait()


def body(sizes, residual, solution, direction, conductance, mass_term, eigen_basis, inverse_eigen_sums,
         element_coarse_index, xxt_values, xxt_blocks, prior_inner):
    stages = group_stages(*sizes)
    sends = sum(len(s) for s in stages)
    lanes = residual.shape[2]
    wide = inverse_eigen_sums.shape[2]
    coarse = xxt_values.shape[1]
    bs = xxt_values.shape[2]
    nb = coarse * sizes[0] * sizes[1] * sizes[2] // bs
    base = cheb_matrix()
    dmat = jnp.asarray(np.concatenate([base, base.T], axis=1))
    dz = jnp.asarray(np.kron(np.eye(lanes // 8, dtype=np.float32), base))
    hbm = pl.BlockSpec(memory_space=pltpu.HBM)
    out = jax.ShapeDtypeStruct(residual.shape, F32)
    ns = len(stages)
    inputs = (residual, solution, direction, conductance, mass_term, eigen_basis, inverse_eigen_sums,
              element_coarse_index, xxt_values, xxt_blocks, prior_inner, dmat, dz)
    scalars = (9, 10)
    held = [(pltpu.SMEM if n in scalars else pltpu.VMEM)(a.shape, a.dtype) for n, a in enumerate(inputs)]
    results = pl.pallas_call(
        functools.partial(kernel, sizes, stages),
        out_shape=(out, out, out),
        in_specs=[hbm] * len(inputs),
        out_specs=(hbm, hbm, hbm),
        scratch_shapes=held + [
            pltpu.SMEM(eigen_basis.shape, F32),
            pltpu.VMEM((2, 8, 256), F32),
            pltpu.VMEM((2, 8, 256), F32),
            pltpu.VMEM((18, 24, wide), F32),
            pltpu.VMEM((2, 16, wide), F32),
            pltpu.VMEM((2, 32, wide), F32),
            pltpu.VMEM((18, 2, 16, wide), F32),
            pltpu.VMEM((20, 2, 16, wide), F32),
            pltpu.VMEM((10, 2, 2, 16, wide), F32),
            pltpu.VMEM((2, 8, 2, 8, lanes), F32),
            pltpu.VMEM((ns, nb, bs), F32),
            pltpu.VMEM((sends, nb, bs), F32),
            pltpu.VMEM((nb, bs), F32),
            pltpu.VMEM((2, 2, 8, 256), F32),
            pltpu.VMEM((2, 2, 8, 256), F32),
            pltpu.VMEM((2, 16, 16, lanes), F32),
            pltpu.VMEM((2, 2, 16, lanes), F32),
            pltpu.VMEM((2, 2, 16, lanes), F32),
            pltpu.VMEM((2, 2, 32, lanes), F32),
            pltpu.VMEM((ns, 8, lanes), F32),
            pltpu.VMEM((sends, 8, lanes), F32),
            pltpu.VMEM(residual.shape, F32),
            pltpu.VMEM(residual.shape, F32),
            pltpu.VMEM(residual.shape, F32),
            pltpu.SemaphoreType.DMA((20,)),
            pltpu.SemaphoreType.DMA((20,)),
            pltpu.SemaphoreType.DMA((sends,)),
            pltpu.SemaphoreType.DMA((sends,)),
            pltpu.SemaphoreType.DMA((sends,)),
            pltpu.SemaphoreType.DMA((sends,)),
            pltpu.SemaphoreType.DMA((len(inputs) + 1,)),
            pltpu.SemaphoreType.DMA((3,)),
        ],
        compiler_params=pltpu.CompilerParams(
            collective_id=0, has_side_effects=True, vmem_limit_bytes=64 * 1024 * 1024
        ),
    )(*inputs)
    return pl.pallas_call(
        write_out,
        out_shape=(out, out, out),
        in_specs=[hbm] * 3,
        out_specs=(hbm, hbm, hbm),
        scratch_shapes=[pltpu.SemaphoreType.DMA((3,))],
        compiler_params=pltpu.CompilerParams(vmem_limit_bytes=64 * 1024 * 1024),
    )(*results)


def solution(mesh):
    grid = P("gx", "gy", "gz")
    in_specs = (
        grid, grid, grid, P(None, "gx", "gy", "gz"), grid, P(), grid, grid,
        P(("gx", "gy", "gz"), None, None), P(("gx", "gy", "gz")), P(),
    )
    sizes = (mesh.shape["gx"], mesh.shape["gy"], mesh.shape["gz"])
    return jax.shard_map(functools.partial(body, sizes), mesh=mesh, in_specs=in_specs,
                         out_specs=(grid, grid, grid), check_vma=False)
```

```python
import functools

import jax
import jax.numpy as jnp
import numpy as np
from jax import lax
from jax.experimental import pallas as pl
from jax.experimental.pallas import tpu as pltpu
from jax.sharding import PartitionSpec as P

MESH = pl.DeviceIdType.MESH
HIGHEST = lax.Precision.HIGHEST
F32 = jnp.float32
BF16 = jnp.bfloat16


def cheb_matrix():
    count = 8
    points = np.cos(np.pi * np.arange(count) / (count - 1))
    signs = np.array([2.0, 1, 1, 1, 1, 1, 1, 2.0]) * (-1.0) ** np.arange(count)
    differ = points[:, None] - points[None, :] + np.eye(count)
    matrix = np.outer(signs, 1.0 / signs) / differ
    matrix = matrix - np.eye(count) * np.sum(matrix, axis=1)[:, None]
    return (0.25 * matrix).astype(np.float32)


NN = (((1,), (0,)), ((), ()))
NT = (((1,), (1,)), ((), ()))
TN = (((0,), (0,)), ((), ()))


def split2(a):
    hi = a.astype(BF16)
    return hi, (a - hi.astype(F32)).astype(BF16)


def dot3(a, b, dims):
    ah, al = split2(a)
    bh, bl = b
    dot = lambda x, y: lax.dot_general(x, y, dims, preferred_element_type=F32)
    return dot(ah, bh) + (dot(ah, bl) + dot(al, bh))


def exact_dot(a, b, dims):
    return lax.dot_general(a, b, dims, precision=HIGHEST, preferred_element_type=F32)


def iota(shape, axis):
    return lax.broadcasted_iota(jnp.int32, shape, axis)


def group_stages(nx, ny, nz):
    if ny * nz <= 8:
        first = [(0, b, c) for b in range(ny) for c in range(nz) if (b, c) != (0, 0)]
        stages = [first]
    else:
        stages = [[(0, 0, c) for c in range(1, nz)], [(0, b, 0) for b in range(1, ny)]]
    return stages + [[(a, 0, 0) for a in range(1, nx)]]


def node_rows(elem, count, low, high):
    rows = [8 * elem - 2] + list(range(8 * elem, 8 * elem + 8)) + [8 * elem + 9]
    return [low if r < 0 else high if r >= 8 * count else r for r in rows]


def kernel(
    sizes,
    stages,
    h_res, h_sol, h_dirn, h_cond, h_mass, h_eb, h_inv, h_idx, h_xv, h_xb, h_prior, h_dmat, h_dz,
    o_sol, o_res, o_dir,
    res, sol, dirn, cond, mass, eb, inv, idx, xv, xb, prior, dmat, dz, eb_s,
    zs, zr, q, ys, yr, ts, inv2, ws, lp, part, aslot, cin,
    zs2, zr2, g2, ys2, xr2, yr2, sc, bslot,
    nsol, nres, ndir, hs, hr, as_, ar, bs_, br, ls, os_,
):
    nx, ny, nz = sizes
    ix, iy, iz = lax.axis_index("gx"), lax.axis_index("gy"), lax.axis_index("gz")
    D = cheb_matrix()
    have = {
        ("x", -1): ix > 0, ("x", 1): ix < nx - 1,
        ("y", -1): iy > 0, ("y", 1): iy < ny - 1,
        ("z", -1): iz > 0, ("z", 1): iz < nz - 1,
    }

    pairs = dict(
        res=(h_res, res), eb=(h_eb, eb), eb_s=(h_eb, eb_s), xv=(h_xv, xv), idx=(h_idx, idx), xb=(h_xb, xb),
        dirn=(h_dirn, dirn), cond=(h_cond, cond), mass=(h_mass, mass), dmat=(h_dmat, dmat), dz=(h_dz, dz),
        inv=(h_inv, inv), sol=(h_sol, sol), prior=(h_prior, prior),
    )
    loads = {name: pltpu.make_async_copy(src, dst, ls.at[n]) for n, (name, (src, dst)) in enumerate(pairs.items())}

    def arrived(*names):
        for name in names:
            loads[name].wait()

    barrier = pltpu.get_barrier_semaphore()
    all_offsets = [o for stage in stages for o in stage]

    def partner(o):
        return (lax.rem(ix + o[0], nx), lax.rem(iy + o[1], ny), lax.rem(iz + o[2], nz))

    corners = {(a % nx, b % ny, 0) for a in (-1, 1) for b in (-1, 1)} - set(all_offsets) - {(0, 0, 0)}
    greeted = all_offsets + sorted(corners)
    for o in greeted:
        pl.semaphore_signal(barrier, inc=1, device_id=partner(o), device_id_type=MESH)

    for copy in loads.values():
        copy.start()

    def message(k, src, dst, dev):
        return pltpu.make_async_remote_copy(
            src_ref=src, dst_ref=dst, send_sem=hs.at[k], recv_sem=hr.at[k],
            device_id=dev, device_id_type=MESH,
        )

    def each(items, act):
        for args in items[None]:
            act(message(*args))
        if len(items) == 1:
            return
        for side in (-1, 1):
            @pl.when(have["x", side])
            def _(side=side):
                for args in items[side]:
                    act(message(*args))

    def both(send, receive):
        return {"send": send, "receive": receive}

    def start(group):
        each(group["send"], lambda m: m.start())

    def wait_recv(group):
        each(group["receive"], lambda m: m.wait_recv())

    def wait_send(group):
        each(group["send"], lambda m: m.wait_send())

    up_y, down_y = lax.rem(iy + 1, ny), lax.rem(iy + ny - 1, ny)
    up_z, down_z = lax.rem(iz + 1, nz), lax.rem(iz + nz - 1, nz)

    def z_items(base, src, dst):
        items = [(base, src.at[1], dst.at[0], (ix, iy, up_z)), (base + 1, src.at[0], dst.at[1], (ix, iy, down_z))]
        return both({None: items}, {None: items})

    def face_items(base, x_src, x_dst, y_src, y_dst, lead):
        if ny == 2:
            ways = [(1 - iy, iy, up_y)]
        else:
            ways = [(1, 0, up_y), (0, 1, down_y)]
        send = {None: [], -1: [], 1: []}
        receive = {None: [], -1: [], 1: []}
        k = base
        for side, slot, near in ways:
            item = (k, y_src.at[side], y_dst.at[(slot,) + lead + (pl.ds(0, 16),)], (ix, near, iz))
            send[None].append(item)
            receive[None].append(item)
            k += 1
        for s in (1, -1):
            item = (k, x_src[s], x_dst[-s], (ix + s, iy, iz))
            send[s].append(item)
            receive[-s].append(item)
            k += 1
            rows, drows = (pl.ds(8, 8), pl.ds(16, 8)) if s == 1 else (pl.ds(0, 8), pl.ds(24, 8))
            for side, slot, near in ways:
                item = (k, y_src.at[(side,) + lead + (rows,)], y_dst.at[(slot,) + lead + (drows,)], (ix + s, near, iz))
                send[s].append(item)
                receive[-s].append(item)
                k += 1
        return both(send, receive)

    full = (slice(None),)
    z1 = z_items(0, zs, zr)
    f1 = face_items(2, {1: q.at[14, pl.ds(0, 16)], -1: q.at[1, pl.ds(0, 16)]},
                    {-1: q.at[16, pl.ds(0, 16)], 1: q.at[17, pl.ds(0, 16)]}, ys, yr, ())
    z2 = z_items(10, zs2, zr2)
    f2 = face_items(12, {1: g2.at[:, 15], -1: g2.at[:, 0]}, {-1: xr2.at[0], 1: xr2.at[1]}, ys2, yr2, full)

    def ring(stage_no, src, slots, ss, rs):
        base = sum(len(s) for s in stages[:stage_no])
        return [
            pltpu.make_async_remote_copy(
                src_ref=src.at[stage_no], dst_ref=slots.at[base + n],
                send_sem=ss.at[base + n], recv_sem=rs.at[base + n],
                device_id=partner(o), device_id_type=MESH,
            )
            for n, o in enumerate(stages[stage_no])
        ]

    def ring_sum(stage_no, src, slots, copies):
        base = sum(len(s) for s in stages[:stage_no])
        total = src[stage_no]
        for n, c in enumerate(copies):
            c.wait_recv()
            total = total + slots[base + n]
        return total

    def or_zero(there, value):
        return jnp.where(there, value, 0.0)

    lanes = res.shape[2]
    wide = q.shape[2]
    elem_z = lanes // 8
    arrived("eb")
    cols = iota((1, wide), 1)
    elem_of = sum((cols >= 10 * k).astype(jnp.int32) for k in range(1, elem_z))
    pick = (iota((10, wide), 0) == cols - 10 * elem_of).astype(F32)
    bwide = exact_dot(eb[...], pick, NN)
    dist = iota((lanes, wide), 0) - 8 * elem_of
    inner_part = jnp.zeros((lanes, wide), F32)
    for i in range(1, 9):
        inner_part = jnp.where(dist == i - 1, bwide[i:i + 1], inner_part)
    zfwd = jnp.where(dist == -2, bwide[0:1], jnp.where(dist == 9, bwide[9:10], inner_part))
    zfwd = split2(zfwd)
    zinv = split2(inner_part)
    rows16 = iota((16, wide), 0)
    zhalo = jnp.where((rows16 == 6) & (cols < 10), bwide[0:1], 0.0)
    zhalo = jnp.where((rows16 == 9) & (cols >= wide - 10), bwide[9:10], zhalo)
    zhalo = split2(zhalo)
    ebt = exact_dot((iota((16, 10), 0) == iota((16, 10), 1)).astype(F32), eb[...], NT)

    arrived("res")
    r2d = res[...].reshape(256, lanes)
    rt = jnp.transpose(r2d)
    zs[0] = rt[0:8]
    zs[1] = rt[lanes - 8:lanes]

    arrived("idx", "xv", "xb")
    expand = (iota((elem_z, lanes), 1) // 8 == iota((elem_z, lanes), 0)).astype(BF16)
    coarse = xv.shape[1]
    masks = []
    acc = jnp.zeros((coarse, lanes), F32)
    for ex in range(2):
        for ey in range(2):
            ids = idx[ex, ey:ey + 1, :].astype(F32).astype(BF16)
            spread_ids = lax.dot_general(ids, expand, NN, preferred_element_type=F32)
            mask = spread_ids == iota((coarse, lanes), 0).astype(F32)
            masks.append(mask)
            block = res[8 * ex:8 * ex + 8, 8 * ey:8 * ey + 8, :]
            colsum = jnp.sum(jnp.sum(block, axis=0), axis=0, keepdims=True)
            acc = acc + jnp.where(mask, colsum, 0.0)
    coarse_res = jnp.sum(acc, axis=1, keepdims=True)
    nb = part.shape[1]
    partial = jnp.zeros((nb, xv.shape[2]), F32)
    rows_b = iota((nb, xv.shape[2]), 0)
    for k in range(xv.shape[0]):
        contrib = jnp.sum(xv[k] * coarse_res, axis=0, keepdims=True)
        partial = partial + jnp.where(rows_b == xb[k], contrib, 0.0)
    part[0] = partial

    pl.semaphore_wait(barrier, len(greeted))
    start(z1)
    a_copies = [ring(0, part, aslot, as_, ar)]
    for c in a_copies[0]:
        c.start()

    own = dot3(r2d, zfwd, NN)
    arrived("inv")
    inv2[...] = jnp.zeros(inv2.shape, F32)
    for ey in range(2):
        inv2[:, ey, 0:10, :] = inv[:, 10 * ey:10 * ey + 10, :]

    wait_recv(z1)
    halo = jnp.concatenate([or_zero(have["z", -1], zr[0]), or_zero(have["z", 1], zr[1])], axis=0)
    qv = (own + dot3(jnp.transpose(halo), zhalo, NN)).reshape(16, 16, wide)
    q[0:16, 0:16, :] = qv
    ys[0] = qv[:, 1, :]
    ys[1] = qv[:, 14, :]
    start(f1)

    arrived("dz", "dirn", "cond", "mass", "dmat")
    dzs = split2(dz[...])

    def local_op(v):
        v4 = v.reshape(2, 8, 16, lanes)
        planes = [v4[:, j] for j in range(8)]
        cg = []
        for a in range(8):
            g = planes[0] * float(D[a, 0])
            for j in range(1, 8):
                g = g + planes[j] * float(D[a, j])
            cg.append(g * cond[0].reshape(2, 8, 16, lanes)[:, a])
        outs = []
        for i in range(8):
            o = cg[0] * float(D[0, i])
            for a in range(1, 8):
                o = o + cg[a] * float(D[a, i])
            outs.append(o)
        total = jnp.stack(outs, axis=1).reshape(16, 16, lanes) + mass[...] * v
        vy = v.reshape(16, 2, 8, lanes)
        g = vy[:, :, 0:1, :] * dmat[:, 0:1]
        for j in range(1, 8):
            g = g + vy[:, :, j:j + 1, :] * dmat[:, j:j + 1]
        g = g * cond[1].reshape(16, 2, 8, lanes)
        o = g[:, :, 0:1, :] * dmat[:, 8:9]
        for j in range(1, 8):
            o = o + g[:, :, j:j + 1, :] * dmat[:, 8 + j:9 + j]
        total = total + o.reshape(16, 16, lanes)
        gz = dot3(v.reshape(256, lanes), dzs, NT) * cond[2].reshape(256, lanes)
        return total + dot3(gz, dzs, NN).reshape(16, 16, lanes)

    dv = dirn[...]
    ld = local_op(dv)
    g2[1] = ld
    ldt = jnp.transpose(ld.reshape(256, lanes))
    zs2[0, 1] = ldt[0:8]
    zs2[1, 1] = ldt[lanes - 8:lanes]
    sc[0] = jnp.zeros((8, lanes), F32)
    sc[0, 2:3, :] = jnp.sum(jnp.sum(dv * ld, axis=0), axis=0, keepdims=True)

    for st in range(1, len(stages)):
        part[st] = ring_sum(st - 1, part, aslot, a_copies[st - 1])
        a_copies.append(ring(st, part, aslot, as_, ar))
        for c in a_copies[st]:
            c.start()

    arrived("eb_s", "sol", "prior")
    wait_recv(f1)
    for n, s in enumerate((-1, 1)):
        q[16 + n, 0:16] = or_zero(have["x", s], q[16 + n, 0:16])
        there = have["y", s]
        q[0:16, 16 + n:17 + n, :] = or_zero(there, yr[n, 0:16]).reshape(16, 1, wide)
        q[16, 16 + n:17 + n, :] = or_zero(there & have["x", -1], yr[n, 22:23])
        q[17, 16 + n:17 + n, :] = or_zero(there & have["x", 1], yr[n, 25:26])
    for ey in range(2):
        t = None
        for j, row in enumerate(node_rows(ey, 2, 16, 17)):
            term = q[:, row:row + 1, :] * ebt[:, j:j + 1]
            t = term if t is None else t + term
        ts[:, ey] = t
    maps = [node_rows(ex, 2, 16, 17) for ex in range(2)]
    planes = [jnp.stack([ts[maps[0][i]], ts[maps[1][i]]]) for i in range(10)]
    inner_acc = None
    for a in range(10):
        u = planes[0] * eb_s[0, a]
        for i in range(1, 10):
            u = u + planes[i] * eb_s[i, a]
        w = u * jnp.stack([inv2[a], inv2[10 + a]])
        ws[a] = w
        term = u * w
        inner_acc = term if inner_acc is None else inner_acc + term
    inner_row = jnp.sum(jnp.sum(inner_acc, axis=(0, 1)), axis=0, keepdims=True)
    inner_local = jnp.sum(inner_row, axis=1, keepdims=True)
    sc[0, 3:4, :] = jnp.where(iota((1, lanes), 1) == 0, inner_local, 0.0)

    back = dot3(ws[...].reshape(640, wide), zinv, NT).reshape(10, 2, 2, 16, lanes)
    for m in range(8):
        o = back[0] * eb_s[m + 1, 0]
        for a in range(1, 10):
            o = o + back[a] * eb_s[m + 1, a]
        y = None
        for a in range(10):
            term = o[:, :, a:a + 1, :] * eb[1:9, a:a + 1]
            y = term if y is None else y + term
        lp[:, m] = y

    last = len(stages) - 1
    coarse_inner = ring_sum(last, part, aslot, a_copies[last])
    cin[...] = coarse_inner
    coarse_square = jnp.sum(jnp.sum(coarse_inner * coarse_inner, axis=0, keepdims=True), axis=1, keepdims=True)
    acc = None
    for k in range(xv.shape[0]):
        term = xv[k] * cin[pl.ds(xb[k], 1), :]
        acc = term if acc is None else acc + term
    coarse_sol = jnp.sum(acc, axis=1, keepdims=True)
    for ex in range(2):
        for ey in range(2):
            row = jnp.sum(jnp.where(masks[2 * ex + ey], coarse_sol, 0.0), axis=0, keepdims=True)
            lp[ex, :, ey] = lp[ex, :, ey] + row
    z = lp[...].reshape(16, 16, lanes)
    lz = local_op(z)
    lzt = jnp.transpose(lz.reshape(256, lanes))
    zs2[0, 0] = lzt[0:8]
    zs2[1, 0] = lzt[lanes - 8:lanes]
    start(z2)
    g2[0] = lz
    sc[0, 0:1, :] = jnp.sum(jnp.sum(z * lz, axis=0), axis=0, keepdims=True)
    sc[0, 1:2, :] = jnp.sum(jnp.sum(z * g2[1], axis=0), axis=0, keepdims=True)
    b_copies = [ring(0, sc, bslot, bs_, br)]
    for c in b_copies[0]:
        c.start()

    lane = iota((256, lanes), 1)
    up = (lane % 8 == 7) & (lane < lanes - 1)
    down = (lane % 8 == 0) & (lane > 0)
    r16 = iota((16, lanes), 0)
    l16 = iota((16, lanes), 1)
    put = (((r16 == 7) & (l16 == 0)) | ((r16 == 8) & (l16 == lanes - 1))).astype(F32)
    inside = []
    for n in range(2):
        v = g2[n].reshape(256, lanes)
        inside.append(v + jnp.where(up, pltpu.roll(v, lanes - 1, 1), 0.0) + jnp.where(down, pltpu.roll(v, 1, 1), 0.0))
    wait_recv(z2)
    for n in range(2):
        halo = jnp.concatenate([or_zero(have["z", -1], zr2[0, n]), or_zero(have["z", 1], zr2[1, n])], axis=0)
        v = (inside[n] + exact_dot(jnp.transpose(halo), put, NN)).reshape(16, 16, lanes)
        g2[n] = v
        ys2[0, n] = v[:, 0, :]
        ys2[1, n] = v[:, 15, :]
    start(f2)
    for st in range(1, len(stages)):
        sc[st] = ring_sum(st - 1, sc, bslot, b_copies[st - 1])
        b_copies.append(ring(st, sc, bslot, bs_, br))
        for c in b_copies[st]:
            c.start()

    wait_recv(f2)
    sub = iota((16, lanes), 0)
    assembled = []
    for n in range(2):
        def along_y(v, low, high):
            return v + jnp.where(sub == 0, low, jnp.where(sub == 7, v[:, 8:9, :], jnp.where(
                sub == 8, v[:, 7:8, :], jnp.where(sub == 15, high, 0.0))))
        ends = [or_zero(have["y", s], yr2[m, n]) for m, s in enumerate((-1, 1))]
        v = along_y(g2[n], ends[0][0:16].reshape(16, 1, lanes), ends[1][0:16].reshape(16, 1, lanes))
        xlo = along_y(xr2[0, n:n + 1], ends[0][23:24].reshape(1, 1, lanes), ends[1][23:24].reshape(1, 1, lanes))
        xhi = along_y(xr2[1, n:n + 1], ends[0][24:25].reshape(1, 1, lanes), ends[1][24:25].reshape(1, 1, lanes))
        xlo = or_zero(have["x", -1], xlo)
        xhi = or_zero(have["x", 1], xhi)
        assembled.append(jnp.concatenate([
            v[0:1] + xlo, v[1:7], v[7:8] + v[8:9], v[8:9] + v[7:8], v[9:15], v[15:16] + xhi], axis=0))

    total = ring_sum(last, sc, bslot, b_copies[last])
    sums = jnp.sum(total, axis=1, keepdims=True)
    inner = sums[3:4] + coarse_square
    ratio = inner / prior[0]
    curvature = sums[0:1] + 2.0 * ratio * sums[1:2] + ratio * ratio * sums[2:3]
    alpha = inner / curvature
    p = lp[...].reshape(16, 16, lanes) + ratio.reshape(1, 1, 1) * dirn[...]
    ndir[...] = p
    saves = [pltpu.make_async_copy(src, dst, os_.at[n]) for n, (src, dst) in enumerate(
        ((nsol, o_sol), (nres, o_res), (ndir, o_dir)))]
    saves[2].start()
    nsol[...] = sol[...] + alpha.reshape(1, 1, 1) * p
    saves[0].start()
    nres[...] = res[...] - alpha.reshape(1, 1, 1) * (assembled[0] + ratio.reshape(1, 1, 1) * assembled[1])

    saves[1].start()
    for group in (z1, f1, z2, f2):
        wait_send(group)
    for copies in a_copies + b_copies:
        for c in copies:
            c.wait_send()
    for copy in saves:
        copy.wait()


def write_out(a, b, c, ao, bo, co, held, load_sems, save_sems):
    loads = [pltpu.make_async_copy(src, held.at[n], load_sems.at[n]) for n, src in enumerate((a, b, c))]
    saves = [pltpu.make_async_copy(held.at[n], dst, save_sems.at[n]) for n, dst in enumerate((ao, bo, co))]
    for copy in loads:
        copy.start()
    for load, save in zip(loads, saves):
        load.wait()
        save.start()
    for copy in saves:
        copy.wait()


def body(sizes, residual, solution, direction, conductance, mass_term, eigen_basis, inverse_eigen_sums,
         element_coarse_index, xxt_values, xxt_blocks, prior_inner):
    stages = group_stages(*sizes)
    sends = sum(len(s) for s in stages)
    lanes = residual.shape[2]
    wide = inverse_eigen_sums.shape[2]
    coarse = xxt_values.shape[1]
    bs = xxt_values.shape[2]
    nb = coarse * sizes[0] * sizes[1] * sizes[2] // bs
    base = cheb_matrix()
    dmat = jnp.asarray(np.concatenate([base, base.T], axis=1))
    dz = jnp.asarray(np.kron(np.eye(lanes // 8, dtype=np.float32), base))
    hbm = pl.BlockSpec(memory_space=pltpu.HBM)
    out = jax.ShapeDtypeStruct(residual.shape, F32)
    ns = len(stages)
    inputs = (residual, solution, direction, conductance, mass_term, eigen_basis, inverse_eigen_sums,
              element_coarse_index, xxt_values, xxt_blocks, prior_inner, dmat, dz)
    scalars = (9, 10)
    held = [(pltpu.SMEM if n in scalars else pltpu.VMEM)(a.shape, a.dtype) for n, a in enumerate(inputs)]
    results = pl.pallas_call(
        functools.partial(kernel, sizes, stages),
        out_shape=(out, out, out),
        in_specs=[hbm] * len(inputs),
        out_specs=(hbm, hbm, hbm),
        scratch_shapes=held + [
            pltpu.SMEM(eigen_basis.shape, F32),
            pltpu.VMEM((2, 8, 256), F32),
            pltpu.VMEM((2, 8, 256), F32),
            pltpu.VMEM((18, 24, wide), F32),
            pltpu.VMEM((2, 16, wide), F32),
            pltpu.VMEM((2, 32, wide), F32),
            pltpu.VMEM((18, 2, 16, wide), F32),
            pltpu.VMEM((20, 2, 16, wide), F32),
            pltpu.VMEM((10, 2, 2, 16, wide), F32),
            pltpu.VMEM((2, 8, 2, 8, lanes), F32),
            pltpu.VMEM((ns, nb, bs), F32),
            pltpu.VMEM((sends, nb, bs), F32),
            pltpu.VMEM((nb, bs), F32),
            pltpu.VMEM((2, 2, 8, 256), F32),
            pltpu.VMEM((2, 2, 8, 256), F32),
            pltpu.VMEM((2, 16, 16, lanes), F32),
            pltpu.VMEM((2, 2, 16, lanes), F32),
            pltpu.VMEM((2, 2, 16, lanes), F32),
            pltpu.VMEM((2, 2, 32, lanes), F32),
            pltpu.VMEM((ns, 8, lanes), F32),
            pltpu.VMEM((sends, 8, lanes), F32),
            pltpu.VMEM(residual.shape, F32),
            pltpu.VMEM(residual.shape, F32),
            pltpu.VMEM(residual.shape, F32),
            pltpu.SemaphoreType.DMA((20,)),
            pltpu.SemaphoreType.DMA((20,)),
            pltpu.SemaphoreType.DMA((sends,)),
            pltpu.SemaphoreType.DMA((sends,)),
            pltpu.SemaphoreType.DMA((sends,)),
            pltpu.SemaphoreType.DMA((sends,)),
            pltpu.SemaphoreType.DMA((len(inputs) + 1,)),
            pltpu.SemaphoreType.DMA((3,)),
        ],
        compiler_params=pltpu.CompilerParams(
            collective_id=0, has_side_effects=True, vmem_limit_bytes=64 * 1024 * 1024
        ),
    )(*inputs)
    return pl.pallas_call(
        write_out,
        out_shape=(out, out, out),
        in_specs=[hbm] * 3,
        out_specs=(hbm, hbm, hbm),
        scratch_shapes=[pltpu.VMEM((3,) + residual.shape, F32), pltpu.SemaphoreType.DMA((3,)),
                        pltpu.SemaphoreType.DMA((3,))],
        compiler_params=pltpu.CompilerParams(vmem_limit_bytes=64 * 1024 * 1024),
    )(*results)


def solution(mesh):
    grid = P("gx", "gy", "gz")
    in_specs = (
        grid, grid, grid, P(None, "gx", "gy", "gz"), grid, P(), grid, grid,
        P(("gx", "gy", "gz"), None, None), P(("gx", "gy", "gz")), P(),
    )
    sizes = (mesh.shape["gx"], mesh.shape["gy"], mesh.shape["gz"])
    return jax.shard_map(functools.partial(body, sizes), mesh=mesh, in_specs=in_specs,
                         out_specs=(grid, grid, grid), check_vma=False)
```

```python
import functools

import jax
import jax.numpy as jnp
import numpy as np
from jax import lax
from jax.experimental import pallas as pl
from jax.experimental.pallas import tpu as pltpu
from jax.sharding import PartitionSpec as P

MESH = pl.DeviceIdType.MESH
HIGHEST = lax.Precision.HIGHEST
F32 = jnp.float32
BF16 = jnp.bfloat16


def cheb_matrix():
    count = 8
    points = np.cos(np.pi * np.arange(count) / (count - 1))
    signs = np.array([2.0, 1, 1, 1, 1, 1, 1, 2.0]) * (-1.0) ** np.arange(count)
    differ = points[:, None] - points[None, :] + np.eye(count)
    matrix = np.outer(signs, 1.0 / signs) / differ
    matrix = matrix - np.eye(count) * np.sum(matrix, axis=1)[:, None]
    return (0.25 * matrix).astype(np.float32)


NN = (((1,), (0,)), ((), ()))
NT = (((1,), (1,)), ((), ()))
TN = (((0,), (0,)), ((), ()))


def split2(a):
    hi = a.astype(BF16)
    return hi, (a - hi.astype(F32)).astype(BF16)


def dot3(a, b, dims):
    ah, al = split2(a)
    bh, bl = b
    dot = lambda x, y: lax.dot_general(x, y, dims, preferred_element_type=F32)
    return dot(ah, bh) + (dot(ah, bl) + dot(al, bh))


def exact_dot(a, b, dims):
    return lax.dot_general(a, b, dims, precision=HIGHEST, preferred_element_type=F32)


def iota(shape, axis):
    return lax.broadcasted_iota(jnp.int32, shape, axis)


def group_stages(nx, ny, nz):
    if ny * nz <= 8:
        first = [(0, b, c) for b in range(ny) for c in range(nz) if (b, c) != (0, 0)]
        stages = [first]
    else:
        stages = [[(0, 0, c) for c in range(1, nz)], [(0, b, 0) for b in range(1, ny)]]
    return stages + [[(a, 0, 0) for a in range(1, nx)]]


def node_rows(elem, count, low, high):
    rows = [8 * elem - 2] + list(range(8 * elem, 8 * elem + 8)) + [8 * elem + 9]
    return [low if r < 0 else high if r >= 8 * count else r for r in rows]


def kernel(
    sizes,
    stages,
    h_res, h_sol, h_dirn, h_cond, h_mass, h_eb, h_inv, h_idx, h_xv, h_xb, h_prior, h_dmat, h_dz,
    o_sol, o_res, o_dir,
    res, sol, dirn, cond, mass, eb, inv, idx, xv, xb, prior, dmat, dz, eb_s,
    zs, zr, q, ys, yr, ts, inv2, ws, lp, part, aslot, cin,
    zs2, zr2, g2, ys2, xr2, yr2, sc, bslot,
    nsol, nres, ndir, hs, hr, as_, ar, bs_, br, ls, os_,
):
    nx, ny, nz = sizes
    ix, iy, iz = lax.axis_index("gx"), lax.axis_index("gy"), lax.axis_index("gz")
    D = cheb_matrix()
    have = {
        ("x", -1): ix > 0, ("x", 1): ix < nx - 1,
        ("y", -1): iy > 0, ("y", 1): iy < ny - 1,
        ("z", -1): iz > 0, ("z", 1): iz < nz - 1,
    }

    pairs = dict(
        res=(h_res, res), eb=(h_eb, eb), eb_s=(h_eb, eb_s), xv=(h_xv, xv), idx=(h_idx, idx), xb=(h_xb, xb),
        dirn=(h_dirn, dirn), cond=(h_cond, cond), mass=(h_mass, mass), dmat=(h_dmat, dmat), dz=(h_dz, dz),
        inv=(h_inv, inv), sol=(h_sol, sol), prior=(h_prior, prior),
    )
    loads = {name: pltpu.make_async_copy(src, dst, ls.at[n]) for n, (name, (src, dst)) in enumerate(pairs.items())}

    def arrived(*names):
        for name in names:
            loads[name].wait()

    barrier = pltpu.get_barrier_semaphore()
    all_offsets = [o for stage in stages for o in stage]

    def partner(o):
        return (lax.rem(ix + o[0], nx), lax.rem(iy + o[1], ny), lax.rem(iz + o[2], nz))

    corners = {(a % nx, b % ny, 0) for a in (-1, 1) for b in (-1, 1)} - set(all_offsets) - {(0, 0, 0)}
    greeted = all_offsets + sorted(corners)
    for o in greeted:
        pl.semaphore_signal(barrier, inc=1, device_id=partner(o), device_id_type=MESH)

    for copy in loads.values():
        copy.start()

    def message(k, src, dst, dev):
        return pltpu.make_async_remote_copy(
            src_ref=src, dst_ref=dst, send_sem=hs.at[k], recv_sem=hr.at[k],
            device_id=dev, device_id_type=MESH,
        )

    def each(items, act):
        for args in items[None]:
            act(message(*args))
        if len(items) == 1:
            return
        for side in (-1, 1):
            @pl.when(have["x", side])
            def _(side=side):
                for args in items[side]:
                    act(message(*args))

    def both(send, receive):
        return {"send": send, "receive": receive}

    def start(group):
        each(group["send"], lambda m: m.start())

    def wait_recv(group):
        each(group["receive"], lambda m: m.wait_recv())

    def wait_send(group):
        each(group["send"], lambda m: m.wait_send())

    up_y, down_y = lax.rem(iy + 1, ny), lax.rem(iy + ny - 1, ny)
    up_z, down_z = lax.rem(iz + 1, nz), lax.rem(iz + nz - 1, nz)

    def z_items(base, src, dst):
        items = [(base, src.at[1], dst.at[0], (ix, iy, up_z)), (base + 1, src.at[0], dst.at[1], (ix, iy, down_z))]
        return both({None: items}, {None: items})

    def face_items(base, x_src, x_dst, y_src, y_dst, lead):
        if ny == 2:
            ways = [(1 - iy, iy, up_y)]
        else:
            ways = [(1, 0, up_y), (0, 1, down_y)]
        send = {None: [], -1: [], 1: []}
        receive = {None: [], -1: [], 1: []}
        k = base
        for side, slot, near in ways:
            item = (k, y_src.at[side], y_dst.at[(slot,) + lead + (pl.ds(0, 16),)], (ix, near, iz))
            send[None].append(item)
            receive[None].append(item)
            k += 1
        for s in (1, -1):
            item = (k, x_src[s], x_dst[-s], (ix + s, iy, iz))
            send[s].append(item)
            receive[-s].append(item)
            k += 1
            rows, drows = (pl.ds(8, 8), pl.ds(16, 8)) if s == 1 else (pl.ds(0, 8), pl.ds(24, 8))
            for side, slot, near in ways:
                item = (k, y_src.at[(side,) + lead + (rows,)], y_dst.at[(slot,) + lead + (drows,)], (ix + s, near, iz))
                send[s].append(item)
                receive[-s].append(item)
                k += 1
        return both(send, receive)

    full = (slice(None),)
    z1 = z_items(0, zs, zr)
    f1 = face_items(2, {1: q.at[14, pl.ds(0, 16)], -1: q.at[1, pl.ds(0, 16)]},
                    {-1: q.at[16, pl.ds(0, 16)], 1: q.at[17, pl.ds(0, 16)]}, ys, yr, ())
    z2 = z_items(10, zs2, zr2)
    f2 = face_items(12, {1: g2.at[:, 15], -1: g2.at[:, 0]}, {-1: xr2.at[0], 1: xr2.at[1]}, ys2, yr2, full)

    def ring(stage_no, src, slots, ss, rs):
        base = sum(len(s) for s in stages[:stage_no])
        return [
            pltpu.make_async_remote_copy(
                src_ref=src.at[stage_no], dst_ref=slots.at[base + n],
                send_sem=ss.at[base + n], recv_sem=rs.at[base + n],
                device_id=partner(o), device_id_type=MESH,
            )
            for n, o in enumerate(stages[stage_no])
        ]

    def ring_sum(stage_no, src, slots, copies):
        base = sum(len(s) for s in stages[:stage_no])
        total = src[stage_no]
        for n, c in enumerate(copies):
            c.wait_recv()
            total = total + slots[base + n]
        return total

    def or_zero(there, value):
        return jnp.where(there, value, 0.0)

    lanes = res.shape[2]
    wide = q.shape[2]
    elem_z = lanes // 8
    arrived("eb")
    cols = iota((1, wide), 1)
    elem_of = sum((cols >= 10 * k).astype(jnp.int32) for k in range(1, elem_z))
    pick = (iota((10, wide), 0) == cols - 10 * elem_of).astype(F32)
    bwide = exact_dot(eb[...], pick, NN)
    dist = iota((lanes, wide), 0) - 8 * elem_of
    inner_part = jnp.zeros((lanes, wide), F32)
    for i in range(1, 9):
        inner_part = jnp.where(dist == i - 1, bwide[i:i + 1], inner_part)
    zfwd = jnp.where(dist == -2, bwide[0:1], jnp.where(dist == 9, bwide[9:10], inner_part))
    zfwd = split2(zfwd)
    zinv = split2(inner_part)
    rows16 = iota((16, wide), 0)
    zhalo = jnp.where((rows16 == 6) & (cols < 10), bwide[0:1], 0.0)
    zhalo = jnp.where((rows16 == 9) & (cols >= wide - 10), bwide[9:10], zhalo)
    zhalo = split2(zhalo)
    ebt = exact_dot((iota((16, 10), 0) == iota((16, 10), 1)).astype(F32), eb[...], NT)

    arrived("res")
    r2d = res[...].reshape(256, lanes)
    rt = jnp.transpose(r2d)
    zs[0] = rt[0:8]
    zs[1] = rt[lanes - 8:lanes]

    arrived("idx", "xv", "xb")
    expand = (iota((elem_z, lanes), 1) // 8 == iota((elem_z, lanes), 0)).astype(BF16)
    coarse = xv.shape[1]
    masks = []
    acc = jnp.zeros((coarse, lanes), F32)
    for ex in range(2):
        for ey in range(2):
            ids = idx[ex, ey:ey + 1, :].astype(F32).astype(BF16)
            spread_ids = lax.dot_general(ids, expand, NN, preferred_element_type=F32)
            mask = spread_ids == iota((coarse, lanes), 0).astype(F32)
            masks.append(mask)
            block = res[8 * ex:8 * ex + 8, 8 * ey:8 * ey + 8, :]
            colsum = jnp.sum(jnp.sum(block, axis=0), axis=0, keepdims=True)
            acc = acc + jnp.where(mask, colsum, 0.0)
    coarse_res = jnp.sum(acc, axis=1, keepdims=True)
    nb = part.shape[1]
    partial = jnp.zeros((nb, xv.shape[2]), F32)
    rows_b = iota((nb, xv.shape[2]), 0)
    for k in range(xv.shape[0]):
        contrib = jnp.sum(xv[k] * coarse_res, axis=0, keepdims=True)
        partial = partial + jnp.where(rows_b == xb[k], contrib, 0.0)
    part[0] = partial

    pl.semaphore_wait(barrier, len(greeted))
    start(z1)
    a_copies = [ring(0, part, aslot, as_, ar)]
    for c in a_copies[0]:
        c.start()

    own = dot3(r2d, zfwd, NN)
    arrived("inv")
    inv2[...] = jnp.zeros(inv2.shape, F32)
    for ey in range(2):
        inv2[:, ey, 0:10, :] = inv[:, 10 * ey:10 * ey + 10, :]

    wait_recv(z1)
    halo = jnp.concatenate([or_zero(have["z", -1], zr[0]), or_zero(have["z", 1], zr[1])], axis=0)
    qv = (own + dot3(jnp.transpose(halo), zhalo, NN)).reshape(16, 16, wide)
    q[0:16, 0:16, :] = qv
    ys[0] = qv[:, 1, :]
    ys[1] = qv[:, 14, :]
    start(f1)

    arrived("dz", "dirn", "cond", "mass", "dmat")
    dzs = split2(dz[...])

    def local_op(v):
        v4 = v.reshape(2, 8, 16, lanes)
        planes = [v4[:, j] for j in range(8)]
        cg = []
        for a in range(8):
            g = planes[0] * float(D[a, 0])
            for j in range(1, 8):
                g = g + planes[j] * float(D[a, j])
            cg.append(g * cond[0].reshape(2, 8, 16, lanes)[:, a])
        outs = []
        for i in range(8):
            o = cg[0] * float(D[0, i])
            for a in range(1, 8):
                o = o + cg[a] * float(D[a, i])
            outs.append(o)
        total = jnp.stack(outs, axis=1).reshape(16, 16, lanes) + mass[...] * v
        vy = v.reshape(16, 2, 8, lanes)
        g = vy[:, :, 0:1, :] * dmat[:, 0:1]
        for j in range(1, 8):
            g = g + vy[:, :, j:j + 1, :] * dmat[:, j:j + 1]
        g = g * cond[1].reshape(16, 2, 8, lanes)
        o = g[:, :, 0:1, :] * dmat[:, 8:9]
        for j in range(1, 8):
            o = o + g[:, :, j:j + 1, :] * dmat[:, 8 + j:9 + j]
        total = total + o.reshape(16, 16, lanes)
        gz = dot3(v.reshape(256, lanes), dzs, NT) * cond[2].reshape(256, lanes)
        return total + dot3(gz, dzs, NN).reshape(16, 16, lanes)

    dv = dirn[...]
    ld = local_op(dv)
    g2[1] = ld
    ldt = jnp.transpose(ld.reshape(256, lanes))
    zs2[0, 1] = ldt[0:8]
    zs2[1, 1] = ldt[lanes - 8:lanes]
    sc[0] = jnp.zeros((8, lanes), F32)
    sc[0, 2:3, :] = jnp.sum(jnp.sum(dv * ld, axis=0), axis=0, keepdims=True)

    for st in range(1, len(stages)):
        part[st] = ring_sum(st - 1, part, aslot, a_copies[st - 1])
        a_copies.append(ring(st, part, aslot, as_, ar))
        for c in a_copies[st]:
            c.start()

    for ey in range(2):
        t = None
        for jj, row in enumerate(node_rows(ey, 2, 16, 17)):
            if row < 16:
                term = q[0:16, row:row + 1, :] * ebt[:, jj:jj + 1]
                t = term if t is None else t + term
        ts[0:16, ey] = t
    arrived("eb_s", "sol", "prior")
    wait_recv(f1)
    for n, s in enumerate((-1, 1)):
        q[16 + n, 0:16] = or_zero(have["x", s], q[16 + n, 0:16])
        there = have["y", s]
        q[0:16, 16 + n:17 + n, :] = or_zero(there, yr[n, 0:16]).reshape(16, 1, wide)
        q[16, 16 + n:17 + n, :] = or_zero(there & have["x", -1], yr[n, 22:23])
        q[17, 16 + n:17 + n, :] = or_zero(there & have["x", 1], yr[n, 25:26])
    for ey in range(2):
        rows = node_rows(ey, 2, 16, 17)
        ends = None
        for jj, row in enumerate(rows):
            col = ebt[:, jj:jj + 1]
            if row >= 16:
                ts[0:16, ey] = ts[0:16, ey] + q[0:16, row:row + 1, :] * col
            term = q[16:18, row:row + 1, :] * col
            ends = term if ends is None else ends + term
        ts[16:18, ey] = ends
    maps = [node_rows(ex, 2, 16, 17) for ex in range(2)]
    planes = [jnp.stack([ts[maps[0][i]], ts[maps[1][i]]]) for i in range(10)]
    inner_acc = None
    for a in range(10):
        u = planes[0] * eb_s[0, a]
        for i in range(1, 10):
            u = u + planes[i] * eb_s[i, a]
        w = u * jnp.stack([inv2[a], inv2[10 + a]])
        ws[a] = w
        term = u * w
        inner_acc = term if inner_acc is None else inner_acc + term
    inner_row = jnp.sum(jnp.sum(inner_acc, axis=(0, 1)), axis=0, keepdims=True)
    inner_local = jnp.sum(inner_row, axis=1, keepdims=True)
    sc[0, 3:4, :] = jnp.where(iota((1, lanes), 1) == 0, inner_local, 0.0)

    back = dot3(ws[...].reshape(640, wide), zinv, NT).reshape(10, 2, 2, 16, lanes)
    for m in range(8):
        o = back[0] * eb_s[m + 1, 0]
        for a in range(1, 10):
            o = o + back[a] * eb_s[m + 1, a]
        y = None
        for a in range(10):
            term = o[:, :, a:a + 1, :] * eb[1:9, a:a + 1]
            y = term if y is None else y + term
        lp[:, m] = y

    last = len(stages) - 1
    coarse_inner = ring_sum(last, part, aslot, a_copies[last])
    cin[...] = coarse_inner
    coarse_square = jnp.sum(jnp.sum(coarse_inner * coarse_inner, axis=0, keepdims=True), axis=1, keepdims=True)
    acc = None
    for k in range(xv.shape[0]):
        term = xv[k] * cin[pl.ds(xb[k], 1), :]
        acc = term if acc is None else acc + term
    coarse_sol = jnp.sum(acc, axis=1, keepdims=True)
    for ex in range(2):
        for ey in range(2):
            row = jnp.sum(jnp.where(masks[2 * ex + ey], coarse_sol, 0.0), axis=0, keepdims=True)
            lp[ex, :, ey] = lp[ex, :, ey] + row
    z = lp[...].reshape(16, 16, lanes)
    lz = local_op(z)
    lzt = jnp.transpose(lz.reshape(256, lanes))
    zs2[0, 0] = lzt[0:8]
    zs2[1, 0] = lzt[lanes - 8:lanes]
    start(z2)
    g2[0] = lz
    sc[0, 0:1, :] = jnp.sum(jnp.sum(z * lz, axis=0), axis=0, keepdims=True)
    sc[0, 1:2, :] = jnp.sum(jnp.sum(z * g2[1], axis=0), axis=0, keepdims=True)
    b_copies = [ring(0, sc, bslot, bs_, br)]
    for c in b_copies[0]:
        c.start()

    lane = iota((256, lanes), 1)
    up = (lane % 8 == 7) & (lane < lanes - 1)
    down = (lane % 8 == 0) & (lane > 0)
    r16 = iota((16, lanes), 0)
    l16 = iota((16, lanes), 1)
    put = (((r16 == 7) & (l16 == 0)) | ((r16 == 8) & (l16 == lanes - 1))).astype(BF16)
    inside = []
    for n in range(2):
        v = g2[n].reshape(256, lanes)
        inside.append(v + jnp.where(up, pltpu.roll(v, lanes - 1, 1), 0.0) + jnp.where(down, pltpu.roll(v, 1, 1), 0.0))
    wait_recv(z2)
    for n in range(2):
        halo = jnp.concatenate([or_zero(have["z", -1], zr2[0, n]), or_zero(have["z", 1], zr2[1, n])], axis=0)
        hh, hl = split2(jnp.transpose(halo))
        placed = lax.dot_general(hh, put, NN, preferred_element_type=F32) + lax.dot_general(
            hl, put, NN, preferred_element_type=F32)
        v = (inside[n] + placed).reshape(16, 16, lanes)
        g2[n] = v
        ys2[0, n] = v[:, 0, :]
        ys2[1, n] = v[:, 15, :]
    start(f2)
    for st in range(1, len(stages)):
        sc[st] = ring_sum(st - 1, sc, bslot, b_copies[st - 1])
        b_copies.append(ring(st, sc, bslot, bs_, br))
        for c in b_copies[st]:
            c.start()

    wait_recv(f2)
    sub = iota((16, lanes), 0)
    assembled = []
    for n in range(2):
        def along_y(v, low, high):
            return v + jnp.where(sub == 0, low, jnp.where(sub == 7, v[:, 8:9, :], jnp.where(
                sub == 8, v[:, 7:8, :], jnp.where(sub == 15, high, 0.0))))
        ends = [or_zero(have["y", s], yr2[m, n]) for m, s in enumerate((-1, 1))]
        v = along_y(g2[n], ends[0][0:16].reshape(16, 1, lanes), ends[1][0:16].reshape(16, 1, lanes))
        xlo = along_y(xr2[0, n:n + 1], ends[0][23:24].reshape(1, 1, lanes), ends[1][23:24].reshape(1, 1, lanes))
        xhi = along_y(xr2[1, n:n + 1], ends[0][24:25].reshape(1, 1, lanes), ends[1][24:25].reshape(1, 1, lanes))
        xlo = or_zero(have["x", -1], xlo)
        xhi = or_zero(have["x", 1], xhi)
        assembled.append(jnp.concatenate([
            v[0:1] + xlo, v[1:7], v[7:8] + v[8:9], v[8:9] + v[7:8], v[9:15], v[15:16] + xhi], axis=0))

    total = ring_sum(last, sc, bslot, b_copies[last])
    sums = jnp.sum(total, axis=1, keepdims=True)
    inner = sums[3:4] + coarse_square
    ratio = inner / prior[0]
    curvature = sums[0:1] + 2.0 * ratio * sums[1:2] + ratio * ratio * sums[2:3]
    alpha = inner / curvature
    p = lp[...].reshape(16, 16, lanes) + ratio.reshape(1, 1, 1) * dirn[...]
    ndir[...] = p
    saves = [pltpu.make_async_copy(src, dst, os_.at[n]) for n, (src, dst) in enumerate(
        ((nsol, o_sol), (nres, o_res), (ndir, o_dir)))]
    saves[2].start()
    nsol[...] = sol[...] + alpha.reshape(1, 1, 1) * p
    saves[0].start()
    nres[...] = res[...] - alpha.reshape(1, 1, 1) * (assembled[0] + ratio.reshape(1, 1, 1) * assembled[1])

    saves[1].start()
    for group in (z1, f1, z2, f2):
        wait_send(group)
    for copies in a_copies + b_copies:
        for c in copies:
            c.wait_send()
    for copy in saves:
        copy.wait()


def write_out(a, b, c, ao, bo, co, held, load_sems, save_sems):
    loads = [pltpu.make_async_copy(src, held.at[n], load_sems.at[n]) for n, src in enumerate((a, b, c))]
    saves = [pltpu.make_async_copy(held.at[n], dst, save_sems.at[n]) for n, dst in enumerate((ao, bo, co))]
    for copy in loads:
        copy.start()
    for load, save in zip(loads, saves):
        load.wait()
        save.start()
    for copy in saves:
        copy.wait()


def body(sizes, residual, solution, direction, conductance, mass_term, eigen_basis, inverse_eigen_sums,
         element_coarse_index, xxt_values, xxt_blocks, prior_inner):
    stages = group_stages(*sizes)
    sends = sum(len(s) for s in stages)
    lanes = residual.shape[2]
    wide = inverse_eigen_sums.shape[2]
    coarse = xxt_values.shape[1]
    bs = xxt_values.shape[2]
    nb = coarse * sizes[0] * sizes[1] * sizes[2] // bs
    base = cheb_matrix()
    dmat = jnp.asarray(np.concatenate([base, base.T], axis=1))
    dz = jnp.asarray(np.kron(np.eye(lanes // 8, dtype=np.float32), base))
    hbm = pl.BlockSpec(memory_space=pltpu.HBM)
    out = jax.ShapeDtypeStruct(residual.shape, F32)
    ns = len(stages)
    inputs = (residual, solution, direction, conductance, mass_term, eigen_basis, inverse_eigen_sums,
              element_coarse_index, xxt_values, xxt_blocks, prior_inner, dmat, dz)
    scalars = (9, 10)
    held = [(pltpu.SMEM if n in scalars else pltpu.VMEM)(a.shape, a.dtype) for n, a in enumerate(inputs)]
    results = pl.pallas_call(
        functools.partial(kernel, sizes, stages),
        out_shape=(out, out, out),
        in_specs=[hbm] * len(inputs),
        out_specs=(hbm, hbm, hbm),
        scratch_shapes=held + [
            pltpu.SMEM(eigen_basis.shape, F32),
            pltpu.VMEM((2, 8, 256), F32),
            pltpu.VMEM((2, 8, 256), F32),
            pltpu.VMEM((18, 24, wide), F32),
            pltpu.VMEM((2, 16, wide), F32),
            pltpu.VMEM((2, 32, wide), F32),
            pltpu.VMEM((18, 2, 16, wide), F32),
            pltpu.VMEM((20, 2, 16, wide), F32),
            pltpu.VMEM((10, 2, 2, 16, wide), F32),
            pltpu.VMEM((2, 8, 2, 8, lanes), F32),
            pltpu.VMEM((ns, nb, bs), F32),
            pltpu.VMEM((sends, nb, bs), F32),
            pltpu.VMEM((nb, bs), F32),
            pltpu.VMEM((2, 2, 8, 256), F32),
            pltpu.VMEM((2, 2, 8, 256), F32),
            pltpu.VMEM((2, 16, 16, lanes), F32),
            pltpu.VMEM((2, 2, 16, lanes), F32),
            pltpu.VMEM((2, 2, 16, lanes), F32),
            pltpu.VMEM((2, 2, 32, lanes), F32),
            pltpu.VMEM((ns, 8, lanes), F32),
            pltpu.VMEM((sends, 8, lanes), F32),
            pltpu.VMEM(residual.shape, F32),
            pltpu.VMEM(residual.shape, F32),
            pltpu.VMEM(residual.shape, F32),
            pltpu.SemaphoreType.DMA((20,)),
            pltpu.SemaphoreType.DMA((20,)),
            pltpu.SemaphoreType.DMA((sends,)),
            pltpu.SemaphoreType.DMA((sends,)),
            pltpu.SemaphoreType.DMA((sends,)),
            pltpu.SemaphoreType.DMA((sends,)),
            pltpu.SemaphoreType.DMA((len(inputs) + 1,)),
            pltpu.SemaphoreType.DMA((3,)),
        ],
        compiler_params=pltpu.CompilerParams(
            collective_id=0, has_side_effects=True, vmem_limit_bytes=64 * 1024 * 1024
        ),
    )(*inputs)
    return pl.pallas_call(
        write_out,
        out_shape=(out, out, out),
        in_specs=[hbm] * 3,
        out_specs=(hbm, hbm, hbm),
        scratch_shapes=[pltpu.VMEM((3,) + residual.shape, F32), pltpu.SemaphoreType.DMA((3,)),
                        pltpu.SemaphoreType.DMA((3,))],
        compiler_params=pltpu.CompilerParams(vmem_limit_bytes=64 * 1024 * 1024),
    )(*results)


def solution(mesh):
    grid = P("gx", "gy", "gz")
    in_specs = (
        grid, grid, grid, P(None, "gx", "gy", "gz"), grid, P(), grid, grid,
        P(("gx", "gy", "gz"), None, None), P(("gx", "gy", "gz")), P(),
    )
    sizes = (mesh.shape["gx"], mesh.shape["gy"], mesh.shape["gz"])
    return jax.shard_map(functools.partial(body, sizes), mesh=mesh, in_specs=in_specs,
                         out_specs=(grid, grid, grid), check_vma=False)
```
